128 devices in a mesh: gz: 8 (over x_hi, z), gy: 16 (over y, x_lo, core).
Axes of the slice: x: 4 (x_hi: 2, x_lo: 2; x = x_hi * 2 + x_lo), y: 4, z: 4, core: 2. Of those that a mesh axis runs over, the one named last changes fastest.
Arguments:
- volume: float32 [96, 128, 256], P('gz', 'gy'), may hold values from -6 to 6
- projector: bfloat16 [4, 1024, 128, 256], P(None, None, 'gy'), may hold values from -0.03125 to 0.03125
- measured: float32 [1024, 96], P(None, 'gz'), may hold values from -6 to 6
- subset: int32 [1], replicated, may hold values from 0 to 1023
- timestep: int32 [1], replicated, may hold values from 100 to 1000
- axial_in: bfloat16 [9, 64, 1], replicated, may hold values from -2 to 2
- axial_bias_in: float32 [64], replicated, may hold values from -3 to 3
- axial_mid: bfloat16 [9, 64, 64], replicated, may hold values from -0.25 to 0.25
- axial_bias_mid: float32 [64], replicated, may hold values from -3 to 3
- axial_out: bfloat16 [9, 1, 64], replicated, may hold values from -0.25 to 0.25
- coronal_in: bfloat16 [9, 64, 1], replicated, may hold values from -2 to 2
- coronal_bias_in: float32 [64], replicated, may hold values from -3 to 3
- coronal_mid: bfloat16 [9, 64, 64], replicated, may hold values from -0.25 to 0.25
- coronal_bias_mid: float32 [64], replicated, may hold values from -3 to 3
- coronal_out: bfloat16 [9, 1, 64], replicated, may hold values from -0.25 to 0.25
Outputs:
- restored: float32 [96, 128, 256], P('gz', 'gy')
- residual: float32 [1024, 96], P('gy', 'gz')
The draws below stay inside these ranges and needn't reach their ends.
All inputs are finite; a program needn't handle non-finite values.
Results may differ from the reference program's by a relative error of at most 0.0075.
Values may be sent and summed in bfloat16 or wider, within the bound.
No kernel may reach another device: no remote copies, remote signals or barrier semaphores. Data moves between devices by JAX's collectives and lax.ppermute only.
A program may use at most 192 MiB of HBM per device.

```python
import jax
import jax.numpy as jnp
from jax import lax

C = 64
RAYS = 1024
X = 256
SUBSETS = 4
NZ = 96
NY = 128


def level_of(rng, shape, shards, least, top_value):
    gain = 1.0
    for dim, blocks in shards:
        heights = jax.random.uniform(jax.random.fold_in(jax.random.fold_in(rng, 6), dim), (blocks,), jnp.float32, least / len(shards), top_value / len(shards))
        gain = gain * jnp.repeat(jnp.exp(heights), shape[dim] // blocks).reshape((-1,) + (1,) * (len(shape) - 1 - dim))
    return gain


def normal_values(key, dims, scale, most, split=(), kind=jnp.bfloat16):
    gain = level_of(key, dims, split, -0.22, 0.18) if split else 1.0
    array = jax.random.normal(key, dims, jnp.float32) * scale * gain
    return jnp.minimum(jnp.maximum(array, -most), most).astype(kind)


def setup_inputs(seed: int = 0) -> dict:
    seeds = jax.random.split(jax.random.key(seed), 16)
    return {
        "volume": normal_values(seeds[0], (NZ, NY, X), 1.0, 6.0, ((0, 8), (1, 16)), jnp.float32),
        "projector": normal_values(seeds[1], (SUBSETS, RAYS, NY, X), (NY * X) ** -0.5, 0.03125, ((2, 16),)),
        "measured": normal_values(seeds[2], (RAYS, NZ), 1.0, 6.0, ((1, 8),), jnp.float32),
        "subset": jax.random.randint(seeds[3], (1,), 0, 256 * SUBSETS).astype(jnp.int32),
        "timestep": jax.random.randint(seeds[4], (1,), 100, 1001).astype(jnp.int32),
        "axial_in": normal_values(seeds[5], (9, C, 1), 9 ** -0.5, 2.0),
        "axial_bias_in": normal_values(seeds[6], (C,), 0.5, 3.0, (), jnp.float32),
        "axial_mid": normal_values(seeds[7], (9, C, C), (9 * C) ** -0.5, 0.25),
        "axial_bias_mid": normal_values(seeds[8], (C,), 0.5, 3.0, (), jnp.float32),
        "axial_out": normal_values(seeds[9], (9, 1, C), (9 * C) ** -0.5, 0.25),
        "coronal_in": normal_values(seeds[10], (9, C, 1), 9 ** -0.5, 2.0),
        "coronal_bias_in": normal_values(seeds[11], (C,), 0.5, 3.0, (), jnp.float32),
        "coronal_mid": normal_values(seeds[12], (9, C, C), (9 * C) ** -0.5, 0.25),
        "coronal_bias_mid": normal_values(seeds[13], (C,), 0.5, 3.0, (), jnp.float32),
        "coronal_out": normal_values(seeds[14], (9, 1, C), (9 * C) ** -0.5, 0.25),
    }


SIGMA_STEP = 0.002
RELAX_TOP = 4.0

def noise_scales(timestep):
    sigma = timestep[0].astype(jnp.float32) * SIGMA_STEP
    scale_in = 1.0 / jnp.sqrt(1.0 + sigma * sigma)
    return (scale_in, sigma * scale_in)

def plane_conv(inputs, taps):
    padded = jnp.pad(inputs, ((0, 0), (1, 1), (1, 1)))
    along = inputs.shape[1]
    across = inputs.shape[2]
    summed = jnp.zeros((taps.shape[1], along, across), jnp.float32)
    for tap_row in range(3):
        for tap_col in range(3):
            shifted = padded[:, tap_row:tap_row + along, tap_col:tap_col + across].astype(jnp.float32)
            kernel = taps[3 * tap_row + tap_col].astype(jnp.float32)
            summed = summed + jnp.einsum('oc,cax->oax', kernel, shifted)
    return summed

def denoise(plane, scale_in, scale_out, first_taps, first_bias, middle_taps, middle_bias, last_taps):
    entry = (plane * scale_in).astype(jnp.bfloat16)[None]
    hidden_one = jnp.maximum(plane_conv(entry, first_taps) + first_bias[:, None, None], 0.0).astype(jnp.bfloat16)
    hidden_two = jnp.maximum(plane_conv(hidden_one, middle_taps) + middle_bias[:, None, None], 0.0).astype(jnp.bfloat16)
    return plane + scale_out * plane_conv(hidden_two, last_taps)[0]

def reference(volume, projector, measured, subset, timestep, axial_in, axial_bias_in, axial_mid, axial_bias_mid, axial_out, coronal_in, coronal_bias_in, coronal_mid, coronal_bias_mid, coronal_out):
    scale_in, scale_out = noise_scales(timestep)
    view = (subset[0] % SUBSETS).astype(jnp.int32)
    epoch = (subset[0] // SUBSETS).astype(jnp.float32)
    relax = RELAX_TOP / (1.0 + epoch / 64.0)

    def axial_plane(plane):
        return denoise(plane, scale_in, scale_out, axial_in, axial_bias_in, axial_mid, axial_bias_mid, axial_out)

    def coronal_plane(plane):
        return denoise(plane, scale_in, scale_out, coronal_in, coronal_bias_in, coronal_mid, coronal_bias_mid, coronal_out)
    axial = lax.map(axial_plane, volume)
    flat = axial.astype(jnp.bfloat16).reshape(NZ, NY * X)
    chosen = lax.dynamic_index_in_dim(projector, view, 0, keepdims=False).reshape(RAYS, NY * X)
    sinogram = lax.dot_general(chosen, flat, (((1,), (1,)), ((), ())), preferred_element_type=jnp.float32)
    residual = measured - sinogram
    rounded = residual.astype(jnp.bfloat16)
    back = lax.dot_general(rounded, chosen, (((0,), (0,)), ((), ())), preferred_element_type=jnp.float32)
    corrected = axial + relax * back.reshape(NZ, NY, X)
    coronal = lax.map(coronal_plane, jnp.transpose(corrected, (1, 0, 2)))
    return (jnp.transpose(coronal, (1, 0, 2)), residual)
```

```python
import functools

import jax
import jax.numpy as jnp
import numpy as np
from jax import lax
from jax.experimental import pallas as pl
from jax.experimental.pallas import tpu as pltpu
from jax.sharding import PartitionSpec as P

SUBSETS = 4
SIGMA_STEP = 0.002
RELAX_TOP = 4.0
HALO = 3
BF = jnp.bfloat16
F32 = jnp.float32
VMEM_LIMIT = 48 << 20


def noise_scales(timestep):
    sigma = timestep[0].astype(F32) * SIGMA_STEP
    scale_in = 1.0 / jnp.sqrt(1.0 + sigma * sigma)
    return (scale_in, sigma * scale_in)


def entry_selector(own, first, second, ones, slots):
    rows = own + 4
    table = np.zeros((2, rows, 11, 3, slots), np.float32)
    for parity in range(2):
        before, after = (second, first) if parity == 0 else (first, second)
        place = (
            [before + k for k in range(HALO)]
            + list(range(own))
            + [after + k for k in range(HALO)]
        )
        for row in range(rows):
            for a in range(3):
                for b in range(3):
                    table[parity, row, 3 * a + b, b, place[row + a]] = 1.0
            table[parity, row, 9, 1, ones] = 1.0
            table[parity, row, 10, 1, ones + 1] = 1.0
    return table.reshape(2, rows, 11, 3 * slots)


def layer_weights(first_taps, first_bias, middle_taps, middle_bias, last_taps, selector, own, index, count):
    rows_one, rows_two = own + 4, own + 2
    base = index * own
    total = count * own
    row_one = base - 2 + jnp.arange(rows_one)
    keep_one = ((row_one >= 0) & (row_one < total)).astype(F32)
    row_two = base - 1 + jnp.arange(rows_two)
    keep_two = ((row_two >= 0) & (row_two < total)).astype(F32)
    high = first_bias.astype(BF)
    low = (first_bias - high.astype(F32)).astype(BF)
    stack = jnp.concatenate([first_taps[:, :, 0], high[None], low[None]], axis=0)
    chosen = lax.dynamic_index_in_dim(jnp.asarray(selector, BF), index % 2, 0, keepdims=False)
    one = jnp.einsum("ko,ikq->ioq", stack, chosen, preferred_element_type=F32)
    one = (one * keep_one[:, None, None]).astype(BF).reshape(rows_one * 64, -1)
    middle = middle_taps.reshape(3, 3, 64, 64).transpose(0, 2, 1, 3).reshape(192, 192)
    padded = -(-own // 8) * 8
    spread = np.zeros((padded, rows_two, 3), np.float32)
    for i in range(own):
        for a in range(3):
            spread[i, i + a, a] = 1.0
    last = jnp.einsum(
        "ija,abc->bijc",
        jnp.asarray(spread, BF),
        last_taps.reshape(3, 3, 64),
        preferred_element_type=F32,
    )
    last = (last * keep_two[None, None, :, None]).astype(BF).reshape(3 * padded, rows_two * 64)
    bias = jnp.broadcast_to(middle_bias[:, None], (64, 256))
    return one, middle, bias, last


def shifted(block):
    lane = lax.broadcasted_iota(jnp.int32, block.shape, 1)
    zero = jnp.zeros((), block.dtype)
    across = block.shape[1]
    left = jnp.where(lane == 0, zero, pltpu.roll(block, 1, 1))
    right = jnp.where(lane == across - 1, zero, pltpu.roll(block, across - 1, 1))
    return left, right


def network(entry, rows_one, one_ref, middle_ref, bias_ref, last_ref, taps_ref, hidden_ref):
    left, right = shifted(entry.astype(F32))
    spread = jnp.concatenate([left.astype(BF), entry, right.astype(BF)], axis=0)
    for row in range(rows_one):
        hidden = jnp.dot(one_ref[row * 64 : (row + 1) * 64, :], spread, preferred_element_type=F32)
        hidden = jnp.maximum(hidden, 0.0).astype(BF)
        left, right = shifted(hidden)
        taps_ref[row * 192 : row * 192 + 64, :] = left
        taps_ref[row * 192 + 64 : row * 192 + 128, :] = hidden
        taps_ref[row * 192 + 128 : row * 192 + 192, :] = right
    bias = bias_ref[...]
    held = []
    for row in range(rows_one):
        held.append(
            jnp.dot(
                middle_ref[...], taps_ref[row * 192 : (row + 1) * 192, :], preferred_element_type=F32
            )
        )
        if row >= 2:
            out = row - 2
            summed = held[out][0:64] + held[out + 1][64:128] + held[out + 2][128:192] + bias
            hidden_ref[out * 64 : (out + 1) * 64, :] = jnp.maximum(summed, 0.0).astype(BF)
    last = jnp.dot(last_ref[...], hidden_ref[...], preferred_element_type=F32)
    rows = last.shape[0] // 3
    left, _ = shifted(last[0:rows])
    _, right = shifted(last[2 * rows :])
    return left + last[rows : 2 * rows] + right


def axial_kernel(
    view_ref,
    scale_ref,
    volume_ref,
    entry_ref,
    one_ref,
    middle_ref,
    bias_ref,
    last_ref,
    fold_ref,
    projector_ref,
    axial_ref,
    partial_ref,
    taps_ref,
    hidden_ref,
    chosen_ref,
    picked_ref,
    sem,
):
    copy = pltpu.make_async_copy(projector_ref.at[view_ref[0]], chosen_ref, sem)
    copy.start()
    axial_ref[...] = jnp.zeros_like(axial_ref)
    scale_out = scale_ref[1]

    def plane(p, carry):
        net = network(entry_ref[p], 12, one_ref, middle_ref, bias_ref, last_ref, taps_ref, hidden_ref)
        value = volume_ref[p] + scale_out * net
        for y in range(8):
            axial_ref[y, pl.ds(p, 1), :] = value[y : y + 1, :]
        return carry

    lax.fori_loop(0, 12, plane, 0)
    copy.wait()
    flat = axial_ref[...].reshape(128, 256).astype(BF)
    lane = lax.broadcasted_iota(jnp.int32, (16, 256), 1) % 8
    for part in range(32):
        product = lax.dot_general(
            flat,
            chosen_ref[part * 256 : (part + 1) * 256, :],
            (((1,), (1,)), ((), ())),
            preferred_element_type=F32,
        )
        picked = product[0:16]
        for y in range(1, 8):
            picked = jnp.where(lane == y, product[y * 16 : (y + 1) * 16], picked)
        row, column = (part // 4) * 16, (part % 4) * 256
        picked_ref[row : row + 16, column : column + 256] = picked
    picked = picked_ref[...]
    high = picked.astype(BF)
    low = (picked - high.astype(F32)).astype(BF)
    fold = fold_ref[...]
    partial_ref[...] = jnp.dot(high, fold, preferred_element_type=F32) + jnp.dot(
        low, fold, preferred_element_type=F32
    )


def back_kernel(
    view_ref,
    place_ref,
    scale_ref,
    measured_ref,
    sinogram_ref,
    axial_ref,
    unfold_ref,
    projector_ref,
    corrected_ref,
    residual_ref,
    chosen_ref,
    held_ref,
    turned_ref,
    sems,
):
    copies = []
    for part in range(8):
        rows = pl.ds(part * 1024, 1024)
        copies.append(
            pltpu.make_async_copy(
                projector_ref.at[view_ref[0], rows], chosen_ref.at[rows], sems.at[part]
            )
        )
        copies[-1].start()
    residual = measured_ref[...] - sinogram_ref[...]
    held_ref[...] = residual
    wide = jnp.dot(residual.astype(BF), unfold_ref[...], preferred_element_type=F32).astype(BF)
    lane = lax.broadcasted_iota(jnp.int32, (16, 1024), 1) % 8
    zero = jnp.zeros((), BF)
    total = jnp.zeros((128, 256), F32)
    for part in range(8):
        rays = wide[part * 16 : (part + 1) * 16]
        spread = jnp.concatenate([jnp.where(lane == y, rays, zero) for y in range(8)], axis=0)
        copies[part].wait()
        total = total + jnp.dot(
            spread, chosen_ref[part * 1024 : (part + 1) * 1024, :], preferred_element_type=F32
        )
    corrected_ref[...] = axial_ref[...] + scale_ref[2] * total.reshape(8, 16, 256)
    block = held_ref[pl.ds(pl.multiple_of(place_ref[0] * 16, 16), 16), :]
    turned_ref[...] = block.T
    start = pl.multiple_of(place_ref[1] * 64, 64)
    residual_ref[...] = turned_ref[pl.ds(start, 64), 0:12]


def coronal_kernel(
    scale_ref,
    corrected_ref,
    entry_ref,
    one_ref,
    middle_ref,
    bias_ref,
    last_ref,
    restored_ref,
    taps_ref,
    hidden_ref,
):
    scale_out = scale_ref[1]

    def plane(p, carry):
        net = network(entry_ref[p], 16, one_ref, middle_ref, bias_ref, last_ref, taps_ref, hidden_ref)
        value = corrected_ref[p] + scale_out * net
        for z in range(12):
            restored_ref[z, pl.ds(p, 1), :] = value[z : z + 1, :]
        return carry

    lax.fori_loop(0, 8, plane, 0)


def vmem():
    return pl.BlockSpec(memory_space=pltpu.VMEM)


def smem():
    return pl.BlockSpec(memory_space=pltpu.SMEM)


def params():
    return pltpu.CompilerParams(vmem_limit_bytes=VMEM_LIMIT)


def inner_pairs(size):
    return [(i, i ^ 1) for i in range(size)]


def outer_pairs(size):
    ups = [(i, i + 1) for i in range(1, size - 1, 2)]
    return ups + [(j, i) for i, j in ups]


def exchange(leading, trailing, axis):
    size = lax.axis_size(axis)
    odd = lax.axis_index(axis) % 2 == 1
    inner = jnp.where(odd, leading, trailing)
    outer = jnp.where(odd, trailing, leading)
    second = lax.ppermute(outer, axis, outer_pairs(size))
    first = lax.ppermute(inner, axis, inner_pairs(size))
    return first, second


def sum_over_gy(partial):
    def partner(value, bits):
        return lax.ppermute(value, "gy", [(i, i ^ bits) for i in range(16)]).astype(F32)

    total = partial
    total = total + partner(total.astype(BF), 1)
    total = total + partner(total.astype(BF), 2)
    sent = total.astype(BF)
    return total + partner(sent, 4) + partner(sent, 8) + partner(sent, 12)


AXIAL_SELECTOR = entry_selector(8, 8, 11, 14, 16)
CORONAL_SELECTOR = entry_selector(12, 16, 19, 30, 32)
FOLD = np.repeat(np.eye(128, dtype=np.float32), 8, axis=0)


def per_device(
    volume,
    projector,
    measured,
    subset,
    timestep,
    axial_in,
    axial_bias_in,
    axial_mid,
    axial_bias_mid,
    axial_out,
    coronal_in,
    coronal_bias_in,
    coronal_mid,
    coronal_bias_mid,
    coronal_out,
):
    scale_in, scale_out = noise_scales(timestep)
    view = subset % SUBSETS
    epoch = (subset[0] // SUBSETS).astype(F32)
    relax = RELAX_TOP / (1.0 + epoch / 64.0)
    scales = jnp.stack([scale_in, scale_out, relax])
    gy, gz = lax.axis_index("gy"), lax.axis_index("gz")
    size_y, size_z = lax.axis_size("gy"), lax.axis_size("gz")
    place = jnp.stack([gy // 2, gy % 2]).astype(jnp.int32)

    entry = (volume * scale_in).astype(BF)
    first, second = exchange(entry[:, :HALO], entry[:, -HALO:], "gy")
    axial_weights = layer_weights(
        axial_in, axial_bias_in, axial_mid, axial_bias_mid, axial_out, AXIAL_SELECTOR, 8, gy, size_y
    )
    coronal_weights = layer_weights(
        coronal_in,
        coronal_bias_in,
        coronal_mid,
        coronal_bias_mid,
        coronal_out,
        CORONAL_SELECTOR,
        12,
        gz,
        size_z,
    )
    flat_projector = projector.reshape(4, 8192, 256)
    turned = jnp.pad(measured.reshape(8, 128, 12).transpose(0, 2, 1), ((0, 0), (0, 4), (0, 0)))
    turned = turned.reshape(128, 128)
    axial_entry = jnp.concatenate([entry, first, second, jnp.ones((12, 2, 256), BF)], axis=1)
    axial, partial = pl.pallas_call(
        axial_kernel,
        name="axial",
        out_shape=(
            jax.ShapeDtypeStruct((8, 16, 256), F32),
            jax.ShapeDtypeStruct((128, 128), F32),
        ),
        in_specs=[smem(), smem()] + [vmem()] * 7 + [pl.BlockSpec(memory_space=pl.ANY)],
        out_specs=(vmem(), vmem()),
        scratch_shapes=[
            pltpu.VMEM((12 * 192, 256), BF),
            pltpu.VMEM((10 * 64, 256), BF),
            pltpu.VMEM((8192, 256), BF),
            pltpu.VMEM((128, 1024), F32),
            pltpu.SemaphoreType.DMA,
        ],
        compiler_params=params(),
    )(view, scales, volume, axial_entry, *axial_weights, jnp.asarray(FOLD, BF), flat_projector)
    sinogram = sum_over_gy(partial)
    corrected, residual = pl.pallas_call(
        back_kernel,
        name="back",
        out_shape=(
            jax.ShapeDtypeStruct((8, 16, 256), F32),
            jax.ShapeDtypeStruct((64, 12), F32),
        ),
        in_specs=[smem(), smem(), smem()] + [vmem()] * 4 + [pl.BlockSpec(memory_space=pl.ANY)],
        out_specs=(vmem(), vmem()),
        scratch_shapes=[
            pltpu.VMEM((8192, 256), BF),
            pltpu.VMEM((128, 128), F32),
            pltpu.VMEM((128, 16), F32),
            pltpu.SemaphoreType.DMA((8,)),
        ],
        compiler_params=params(),
    )(view, place, scales, turned, sinogram, axial, jnp.asarray(FOLD.T, BF), flat_projector)
    entry = (corrected * scale_in).astype(BF)
    first, second = exchange(entry[:, :HALO], entry[:, 12 - HALO : 12], "gz")
    coronal_entry = jnp.concatenate(
        [entry, first, second, jnp.zeros((8, 8, 256), BF), jnp.ones((8, 2, 256), BF)], axis=1
    )
    restored = pl.pallas_call(
        coronal_kernel,
        name="coronal",
        out_shape=jax.ShapeDtypeStruct((12, 8, 256), F32),
        in_specs=[smem()] + [vmem()] * 6,
        out_specs=vmem(),
        scratch_shapes=[
            pltpu.VMEM((16 * 192, 256), BF),
            pltpu.VMEM((14 * 64, 256), BF),
        ],
        compiler_params=params(),
    )(scales, corrected, coronal_entry, *coronal_weights)
    return (restored, residual)


def solution(mesh):
    in_specs = (
        P("gz", "gy", None),
        P(None, None, "gy", None),
        P(None, "gz"),
    ) + (P(),) * 12
    out_specs = (P("gz", "gy", None), P("gy", "gz"))
    return jax.shard_map(
        per_device, mesh=mesh, in_specs=in_specs, out_specs=out_specs, check_vma=False
    )
```

```python
import jax
import jax.numpy as jnp
from jax import lax
from jax.experimental import pallas as pl
from jax.experimental.pallas import tpu as pltpu
from jax.sharding import PartitionSpec as P

SUBSETS = 4
SIGMA_STEP = 0.002
RELAX_TOP = 4.0
HALO = 3
PLANES = 4
BF = jnp.bfloat16
F32 = jnp.float32
AXIAL = (8, 8, 11, 14, 16)
CORONAL = (12, 16, 19, 22, 24)


def noise_scales(timestep_ref):
    sigma = jnp.full((1, 256), timestep_ref[0], jnp.int32).astype(F32) * SIGMA_STEP
    scale_in = 1.0 / jnp.sqrt(1.0 + sigma * sigma)
    return (scale_in, sigma * scale_in)


def relaxation(subset_ref):
    epoch = jnp.full((1, 256), subset_ref[0] // SUBSETS, jnp.int32).astype(F32)
    return RELAX_TOP / (1.0 + epoch / 64.0)


def iota(shape, dim):
    return lax.broadcasted_iota(jnp.int32, shape, dim)


def last_rows(own):
    return -(-3 * (-(-own // 8) * 8) // 16) * 16


def build_weights(layout, index, count, first_taps, first_bias, middle_bias, last_taps, middle_taps_ref, outs):
    own, first, second, ones, slots = layout
    one_ref, middle_ref, bias_ref, last_ref = outs
    rows_one, rows_two = own + 4, own + 2
    total = count * own
    odd = index % 2 == 1
    before = jnp.where(odd, first, second)
    after = jnp.where(odd, second, first)

    def keep(row):
        place = index * own + row
        return jnp.where((place >= 0) & (place < total), 1.0, 0.0).astype(F32)

    def slot(row):
        if row < HALO:
            return before + row
        if row < own + HALO:
            return row - HALO
        return after + row - own - HALO

    rows = jnp.concatenate([first_taps, first_bias, middle_bias, jnp.zeros((5, 64), F32)], axis=0)
    high = rows.astype(BF)
    rest = rows - high.astype(F32)
    middle = rest.astype(BF)
    low = (rest - middle.astype(F32)).astype(BF)
    stack = jnp.concatenate([high, middle, low], axis=0)
    picks = jnp.where(iota((48, 11 * 128), 0) % 16 == iota((48, 11 * 128), 1) // 128, 1.0, 0.0)
    spread = lax.dot_general(
        stack, picks.astype(BF), (((0,), (0,)), ((), ())), preferred_element_type=F32
    )
    columns = [spread[:, k * 128 : (k + 1) * 128] for k in range(11)]
    bias_ref[:, 0:128] = columns[10]
    bias_ref[:, 128:256] = columns[10]
    bias_high = columns[9].astype(BF).astype(F32)
    bias_low = columns[9] - bias_high
    lane = iota((64, 128), 1)
    for row in range(rows_one):
        block = jnp.where(lane == slots + ones, bias_high, 0.0)
        block = jnp.where(lane == slots + ones + 1, bias_low, block)
        for a in range(3):
            for b in range(3):
                block = jnp.where(lane == b * slots + slot(row + a), columns[3 * a + b], block)
        one_ref[row * 64 : (row + 1) * 64, :] = (block * keep(row - 2)).astype(BF)
    padded = last_rows(own)
    band = -(-own // 8) * 8
    sublane = iota((padded, 64), 0)
    for row in range(rows_two):
        block = jnp.zeros((padded, 64), F32)
        for a in range(3):
            if 0 <= row - a < own:
                for b in range(3):
                    tap = last_taps[3 * a + b : 3 * a + b + 1, :]
                    block = jnp.where(sublane == b * band + row - a, tap, block)
        last_ref[:, row * 64 : (row + 1) * 64] = (block * keep(row - 1)).astype(BF)
    middle_ref[...] = jnp.zeros_like(middle_ref)
    for out in range(2):
        for a in range(3):
            for b in range(3):
                column = (out + a) * 192 + b * 64
                middle_ref[out * 64 : (out + 1) * 64, column : column + 64] = middle_taps_ref[3 * a + b]


def build_from(layout, index, count, raw, outs):
    first_taps, first_bias, middle_bias, last_taps, middle_taps_ref = raw
    build_weights(
        layout,
        index,
        count,
        first_taps[...].astype(F32),
        first_bias[...],
        middle_bias[...],
        last_taps[...].astype(F32),
        middle_taps_ref,
        outs,
    )


def prepare_kernel(*refs):
    raw, measured_ref, outs, turned_ref = refs[0:5], refs[5], refs[6:10], refs[10]
    build_from(CORONAL, lax.axis_index("gz"), 8, raw, outs)
    turned_ref[...] = jnp.zeros_like(turned_ref)
    for part in range(8):
        turned_ref[part * 16 : part * 16 + 12, :] = measured_ref[:, part * 128 : (part + 1) * 128]


def weight_shapes(own):
    return [
        (((own + 4) * 64, 128), BF),
        ((128, 768), BF),
        ((64, 256), F32),
        ((last_rows(own), (own + 2) * 64), BF),
    ]


def shifted(block):
    lane = lax.broadcasted_iota(jnp.int32, block.shape, 1)
    zero = jnp.zeros((), block.dtype)
    across = block.shape[1]
    left = jnp.where(lane == 0, zero, pltpu.roll(block, 1, 1))
    right = jnp.where(lane == across - 1, zero, pltpu.roll(block, across - 1, 1))
    return left, right


def spread_entry(own, first, second):
    rows = [own, first, second, jnp.ones((2, own.shape[1]), F32)]
    entry = jnp.concatenate(rows, axis=0)
    left, right = shifted(entry)
    return jnp.concatenate([left, entry, right], axis=0).astype(BF)


def layer_one(spread, rows_one, one_ref, taps_ref):
    depth = spread.shape[0]
    for row in range(rows_one):
        hidden = jnp.dot(
            one_ref[row * 64 : (row + 1) * 64, 0:depth], spread, preferred_element_type=F32
        )
        hidden = jnp.maximum(hidden, 0.0).astype(BF)
        left, right = shifted(hidden)
        taps_ref[row * 192 : row * 192 + 64, :] = left
        taps_ref[row * 192 + 64 : row * 192 + 128, :] = hidden
        taps_ref[row * 192 + 128 : row * 192 + 192, :] = right


def layer_two(rows_two, middle_ref, bias_ref, taps_ref, hidden_ref):
    bias = bias_ref[...]
    for row in range(0, rows_two, 2):
        summed = jnp.dot(
            middle_ref[...], taps_ref[row * 192 : (row + 4) * 192, :], preferred_element_type=F32
        )
        for k in range(2):
            value = jnp.maximum(summed[k * 64 : (k + 1) * 64] + bias, 0.0)
            hidden_ref[(row + k) * 64 : (row + k + 1) * 64, :] = value.astype(BF)


def layer_three(rows, last_ref, hidden_ref):
    last = jnp.dot(last_ref[...], hidden_ref[...], preferred_element_type=F32)
    left, _ = shifted(last[0:rows])
    _, right = shifted(last[2 * rows : 3 * rows])
    return left + last[rows : 2 * rows] + right


def networks(entries, own, weights, scratch):
    one_ref, middle_ref, bias_ref, last_ref = weights
    taps, hidden = scratch[0:PLANES], scratch[PLANES : 2 * PLANES]
    for k in range(PLANES):
        layer_one(spread_entry(*entries[k]), own + 4, one_ref, taps[k])
    for k in range(PLANES):
        layer_two(own + 2, middle_ref, bias_ref, taps[k], hidden[k])
    return [layer_three(-(-own // 8) * 8, last_ref, hidden[k]) for k in range(PLANES)]


def network_scratch(own):
    return [pltpu.VMEM(((own + 4) * 192, 256), BF)] * PLANES + [
        pltpu.VMEM(((own + 2) * 64, 256), BF)
    ] * PLANES


def axial_kernel(
    subset_ref,
    timestep_ref,
    volume_ref,
    first_ref,
    second_ref,
    taps_in_ref,
    bias_in_ref,
    bias_mid_ref,
    taps_out_ref,
    taps_mid_ref,
    projector_ref,
    axial_ref,
    partial_ref,
    sent_ref,
    chosen_ref,
    picked_ref,
    sem,
    *scratch,
):
    copy = pltpu.make_async_copy(projector_ref.at[subset_ref[0] % SUBSETS], chosen_ref, sem)
    copy.start()
    weights, scratch = scratch[0:4], scratch[4:]
    raw = (taps_in_ref, bias_in_ref, bias_mid_ref, taps_out_ref, taps_mid_ref)
    build_from(AXIAL, lax.axis_index("gy"), 16, raw, weights)
    axial_ref[...] = jnp.zeros_like(axial_ref)
    scale_in, scale_out = noise_scales(timestep_ref)

    def planes(step, carry):
        entries = []
        for k in range(PLANES):
            p = step * PLANES + k
            entries.append((volume_ref[p] * scale_in, first_ref[p] * scale_in, second_ref[p] * scale_in))
        nets = networks(entries, 8, weights, scratch)
        for k in range(PLANES):
            p = step * PLANES + k
            value = volume_ref[p] + scale_out * nets[k]
            for y in range(8):
                axial_ref[y, pl.ds(p, 1), :] = value[y : y + 1, :]
        return carry

    lax.fori_loop(0, 12 // PLANES, planes, 0)
    copy.wait()
    flat = axial_ref[...].reshape(128, 256).astype(BF)
    lane = lax.broadcasted_iota(jnp.int32, (16, 256), 1) % 8
    for part in range(32):
        product = lax.dot_general(
            flat,
            chosen_ref[part * 256 : (part + 1) * 256, :],
            (((1,), (1,)), ((), ())),
            preferred_element_type=F32,
        )
        picked = product[0:16]
        for y in range(1, 8):
            picked = jnp.where(lane == y, product[y * 16 : (y + 1) * 16], picked)
        row, column = (part // 4) * 16, (part % 4) * 256
        picked_ref[row : row + 16, column : column + 256] = picked
    picked = picked_ref[...]
    high = picked.astype(BF)
    low = (picked - high.astype(F32)).astype(BF)
    fold = jnp.where(iota((1024, 128), 0) // 8 == iota((1024, 128), 1), 1.0, 0.0).astype(BF)
    partial = jnp.dot(high, fold, preferred_element_type=F32) + jnp.dot(
        low, fold, preferred_element_type=F32
    )
    partial_ref[...] = partial
    sent_ref[...] = partial.astype(BF)


def back_kernel(
    subset_ref,
    measured_ref,
    sinogram_ref,
    axial_ref,
    projector_ref,
    corrected_ref,
    residual_ref,
    chosen_ref,
    held_ref,
    sems,
):
    copies = []
    for part in range(8):
        rows = pl.ds(part * 1024, 1024)
        copies.append(
            pltpu.make_async_copy(
                projector_ref.at[subset_ref[0] % SUBSETS, rows], chosen_ref.at[rows], sems.at[part]
            )
        )
        copies[-1].start()
    residual = measured_ref[...] - sinogram_ref[...]
    held_ref[...] = residual
    unfold = jnp.where(iota((128, 1024), 1) // 8 == iota((128, 1024), 0), 1.0, 0.0).astype(BF)
    wide = jnp.dot(residual.astype(BF), unfold, preferred_element_type=F32).astype(BF)
    lane = lax.broadcasted_iota(jnp.int32, (16, 1024), 1) % 8
    zero = jnp.zeros((), BF)
    total = jnp.zeros((128, 256), F32)
    for part in range(8):
        rays = wide[part * 16 : (part + 1) * 16]
        spread = jnp.concatenate([jnp.where(lane == y, rays, zero) for y in range(8)], axis=0)
        copies[part].wait()
        total = total + jnp.dot(
            spread, chosen_ref[part * 1024 : (part + 1) * 1024, :], preferred_element_type=F32
        )
    corrected_ref[...] = axial_ref[...] + (relaxation(subset_ref) * total).reshape(8, 16, 256)
    index = lax.axis_index("gy")
    block = held_ref[pl.ds(pl.multiple_of((index // 2) * 16, 16), 16), :]
    residual_ref[...] = jnp.where(index % 2 == 1, block[0:12, 64:128], block[0:12, 0:64])


def coronal_kernel(
    timestep_ref,
    corrected_ref,
    first_ref,
    second_ref,
    one_ref,
    middle_ref,
    bias_ref,
    last_ref,
    restored_ref,
    *scratch,
):
    scale_in, scale_out = noise_scales(timestep_ref)
    weights = (one_ref, middle_ref, bias_ref, last_ref)

    def planes(step, carry):
        entries = []
        for k in range(PLANES):
            p = step * PLANES + k
            entries.append((corrected_ref[p] * scale_in, first_ref[p] * scale_in, second_ref[p] * scale_in))
        nets = networks(entries, 12, weights, scratch)
        for k in range(PLANES):
            p = step * PLANES + k
            value = corrected_ref[p] + scale_out * nets[k]
            for z in range(12):
                restored_ref[z, pl.ds(p, 1), :] = value[z : z + 1, :]
        return carry

    lax.fori_loop(0, 8 // PLANES, planes, 0)


def vmem():
    return pl.BlockSpec(memory_space=pltpu.VMEM)


def hbm():
    return pl.BlockSpec(memory_space=pltpu.HBM)


def smem():
    return pl.BlockSpec(memory_space=pltpu.SMEM)


def params(limit):
    return pltpu.CompilerParams(vmem_limit_bytes=limit << 20)


def inner_pairs(size):
    return [(i, i ^ 1) for i in range(size)]


def outer_pairs(size):
    ups = [(i, i + 1) for i in range(1, size - 1, 2)]
    return ups + [(j, i) for i, j in ups]


def exchange(leading, trailing, axis, ordered):
    size = lax.axis_size(axis)
    odd = lax.axis_index(axis) % 2 == 1
    inner = jnp.where(odd, leading, trailing)
    outer = jnp.where(odd, trailing, leading)
    first = lax.ppermute(inner, axis, inner_pairs(size))
    if ordered:
        first, outer = lax.optimization_barrier((first, outer))
    second = lax.ppermute(outer, axis, outer_pairs(size))
    return first, second


def sum_over_gy(partial, sent, axial):
    def partner(value, bits):
        return lax.ppermute(value, "gy", [(i, i ^ bits) for i in range(16)]).astype(F32)

    total = partial + partner(sent, 1)
    total = total + partner(total.astype(BF), 2)
    sent, axial = lax.optimization_barrier((total.astype(BF), axial))
    total = total + partner(sent, 4)
    return total + partner(total.astype(BF), 8), axial


def per_device(
    volume,
    projector,
    measured,
    subset,
    timestep,
    axial_in,
    axial_bias_in,
    axial_mid,
    axial_bias_mid,
    axial_out,
    coronal_in,
    coronal_bias_in,
    coronal_mid,
    coronal_bias_mid,
    coronal_out,
):
    first, second = exchange(volume[:, :HALO], volume[:, -HALO:], "gy", False)
    prepared = pl.pallas_call(
        prepare_kernel,
        name="prepare",
        out_shape=tuple(jax.ShapeDtypeStruct(*shape) for shape in weight_shapes(12))
        + (jax.ShapeDtypeStruct((128, 128), F32),),
        in_specs=[vmem()] * 6,
        out_specs=(vmem(),) * 5,
        compiler_params=params(48),
        cost_estimate=pl.CostEstimate(flops=1000000, bytes_accessed=3000000, transcendentals=0),
    )(
        coronal_in[:, :, 0],
        coronal_bias_in[None],
        coronal_bias_mid[None],
        coronal_out[:, 0, :],
        coronal_mid,
        measured.T,
    )
    coronal_weights, turned = prepared[0:4], prepared[4]
    flat_projector = projector.reshape(4, 8192, 256)
    axial, partial, sent = pl.pallas_call(
        axial_kernel,
        name="axial",
        out_shape=(
            jax.ShapeDtypeStruct((8, 16, 256), F32),
            jax.ShapeDtypeStruct((128, 128), F32),
            jax.ShapeDtypeStruct((128, 128), BF),
        ),
        in_specs=[smem()] * 2 + [vmem()] * 8 + [hbm()],
        out_specs=(vmem(),) * 3,
        scratch_shapes=[
            pltpu.VMEM((8192, 256), BF),
            pltpu.VMEM((128, 1024), F32),
            pltpu.SemaphoreType.DMA,
        ]
        + [pltpu.VMEM(*shape) for shape in weight_shapes(8)]
        + network_scratch(8),
        compiler_params=params(60),
    )(
        subset,
        timestep,
        volume,
        first,
        second,
        axial_in[:, :, 0],
        axial_bias_in[None],
        axial_bias_mid[None],
        axial_out[:, 0, :],
        axial_mid,
        flat_projector,
    )
    zero = timestep[0].astype(F32) * 0.0
    partial = lax.optimization_barrier(partial + zero)
    sinogram, axial = sum_over_gy(partial, sent, axial)
    axial = lax.optimization_barrier(axial + zero)
    corrected, residual = pl.pallas_call(
        back_kernel,
        name="back",
        out_shape=(
            jax.ShapeDtypeStruct((8, 16, 256), F32),
            jax.ShapeDtypeStruct((12, 64), F32),
        ),
        in_specs=[smem()] + [vmem()] * 3 + [hbm()],
        out_specs=(vmem(), vmem()),
        scratch_shapes=[
            pltpu.VMEM((8192, 256), BF),
            pltpu.VMEM((128, 128), F32),
            pltpu.SemaphoreType.DMA((8,)),
        ],
        compiler_params=params(48),
    )(subset, turned, sinogram, axial, flat_projector)
    first, second = exchange(corrected[:, :HALO], corrected[:, 12 - HALO : 12], "gz", False)
    restored = pl.pallas_call(
        coronal_kernel,
        name="coronal",
        out_shape=jax.ShapeDtypeStruct((12, 8, 256), F32),
        in_specs=[smem()] + [vmem()] * 7,
        out_specs=vmem(),
        scratch_shapes=network_scratch(12),
        compiler_params=params(48),
    )(timestep, corrected, first, second, *coronal_weights)
    return (restored, residual.T)


def solution(mesh):
    in_specs = (
        P("gz", "gy", None),
        P(None, None, "gy", None),
        P(None, "gz"),
    ) + (P(),) * 12
    out_specs = (P("gz", "gy", None), P("gy", "gz"))
    return jax.shard_map(
        per_device, mesh=mesh, in_specs=in_specs, out_specs=out_specs, check_vma=False
    )
```

```python
import jax
import jax.numpy as jnp
from jax import lax
from jax.experimental import pallas as pl
from jax.experimental.pallas import tpu as pltpu
from jax.sharding import PartitionSpec as P

SUBSETS = 4
SIGMA_STEP = 0.002
RELAX_TOP = 4.0
HALO = 3
PLANES = 4
BF = jnp.bfloat16
F32 = jnp.float32
AXIAL = (8, 8, 11, 14, 16)
CORONAL = (12, 16, 19, 22, 24)


def noise_scales(timestep_ref):
    sigma = jnp.full((1, 256), timestep_ref[0], jnp.int32).astype(F32) * SIGMA_STEP
    scale_in = 1.0 / jnp.sqrt(1.0 + sigma * sigma)
    return (scale_in, sigma * scale_in)


def relaxation(subset_ref):
    epoch = jnp.full((1, 256), subset_ref[0] // SUBSETS, jnp.int32).astype(F32)
    return RELAX_TOP / (1.0 + epoch / 64.0)


def iota(shape, dim):
    return lax.broadcasted_iota(jnp.int32, shape, dim)


def last_rows(own):
    return -(-3 * (-(-own // 8) * 8) // 16) * 16


def build_weights(layout, index, count, first_taps, first_bias, middle_bias, last_taps, middle_taps_ref, outs):
    own, first, second, ones, slots = layout
    one_ref, middle_ref, bias_ref, last_ref = outs
    rows_one, rows_two = own + 4, own + 2
    total = count * own
    odd = index % 2 == 1
    before = jnp.where(odd, first, second)
    after = jnp.where(odd, second, first)

    def keep(row):
        place = index * own + row
        return jnp.where((place >= 0) & (place < total), 1.0, 0.0).astype(F32)

    def slot(row):
        if row < HALO:
            return before + row
        if row < own + HALO:
            return row - HALO
        return after + row - own - HALO

    rows = jnp.concatenate([first_taps, first_bias, middle_bias, jnp.zeros((5, 64), F32)], axis=0)
    high = rows.astype(BF)
    rest = rows - high.astype(F32)
    middle = rest.astype(BF)
    low = (rest - middle.astype(F32)).astype(BF)
    stack = jnp.concatenate([high, middle, low], axis=0)
    picks = jnp.where(iota((48, 11 * 128), 0) % 16 == iota((48, 11 * 128), 1) // 128, 1.0, 0.0)
    spread = lax.dot_general(
        stack, picks.astype(BF), (((0,), (0,)), ((), ())), preferred_element_type=F32
    )
    columns = [spread[:, k * 128 : (k + 1) * 128] for k in range(11)]
    bias_ref[:, 0:128] = columns[10]
    bias_ref[:, 128:256] = columns[10]
    bias_high = columns[9].astype(BF).astype(F32)
    bias_low = columns[9] - bias_high
    lane = iota((64, 128), 1)
    for row in range(rows_one):
        block = jnp.where(lane == slots + ones, bias_high, 0.0)
        block = jnp.where(lane == slots + ones + 1, bias_low, block)
        for a in range(3):
            for b in range(3):
                block = jnp.where(lane == b * slots + slot(row + a), columns[3 * a + b], block)
        one_ref[row * 64 : (row + 1) * 64, :] = (block * keep(row - 2)).astype(BF)
    padded = last_rows(own)
    band = -(-own // 8) * 8
    sublane = iota((padded, 64), 0)
    for row in range(rows_two):
        block = jnp.zeros((padded, 64), F32)
        for a in range(3):
            if 0 <= row - a < own:
                for b in range(3):
                    tap = last_taps[3 * a + b : 3 * a + b + 1, :]
                    block = jnp.where(sublane == b * band + row - a, tap, block)
        last_ref[:, row * 64 : (row + 1) * 64] = (block * keep(row - 1)).astype(BF)
    middle_ref[...] = jnp.zeros_like(middle_ref)
    for out in range(2):
        for a in range(3):
            for b in range(3):
                column = (out + a) * 192 + b * 64
                middle_ref[out * 64 : (out + 1) * 64, column : column + 64] = middle_taps_ref[3 * a + b]


def build_from(layout, index, count, raw, outs):
    first_taps, first_bias, middle_bias, last_taps, middle_taps_ref = raw
    build_weights(
        layout,
        index,
        count,
        first_taps[...].astype(F32),
        first_bias[...],
        middle_bias[...],
        last_taps[...].astype(F32),
        middle_taps_ref,
        outs,
    )


def prepare_kernel(*refs):
    raw, measured_ref, outs, turned_ref = refs[0:5], refs[5], refs[6:10], refs[10]
    build_from(CORONAL, lax.axis_index("gz"), 8, raw, outs)
    turned_ref[...] = jnp.zeros_like(turned_ref)
    for part in range(8):
        turned_ref[part * 16 : part * 16 + 12, :] = measured_ref[:, part * 128 : (part + 1) * 128]


def weight_shapes(own):
    return [
        (((own + 4) * 64, 128), BF),
        ((128, 768), BF),
        ((64, 256), F32),
        ((last_rows(own), (own + 2) * 64), BF),
    ]


def shifted(block):
    lane = lax.broadcasted_iota(jnp.int32, block.shape, 1)
    zero = jnp.zeros((), block.dtype)
    across = block.shape[1]
    left = jnp.where(lane == 0, zero, pltpu.roll(block, 1, 1))
    right = jnp.where(lane == across - 1, zero, pltpu.roll(block, across - 1, 1))
    return left, right


def spread_entry(own, first, second):
    rows = [own, first, second, jnp.ones((2, own.shape[1]), F32)]
    entry = jnp.concatenate(rows, axis=0)
    left, right = shifted(entry)
    return jnp.concatenate([left, entry, right], axis=0).astype(BF)


def layer_one(spread, rows_one, one_ref, taps_ref):
    depth = spread.shape[0]
    for row in range(rows_one):
        hidden = jnp.dot(
            one_ref[row * 64 : (row + 1) * 64, 0:depth], spread, preferred_element_type=F32
        )
        hidden = jnp.maximum(hidden, 0.0).astype(BF)
        left, right = shifted(hidden)
        taps_ref[row * 192 : row * 192 + 64, :] = left
        taps_ref[row * 192 + 64 : row * 192 + 128, :] = hidden
        taps_ref[row * 192 + 128 : row * 192 + 192, :] = right


def layer_two(rows_two, middle_ref, bias_ref, taps_ref, hidden_ref):
    bias = bias_ref[...]
    for row in range(0, rows_two, 2):
        summed = jnp.dot(
            middle_ref[...], taps_ref[row * 192 : (row + 4) * 192, :], preferred_element_type=F32
        )
        for k in range(2):
            value = jnp.maximum(summed[k * 64 : (k + 1) * 64] + bias, 0.0)
            hidden_ref[(row + k) * 64 : (row + k + 1) * 64, :] = value.astype(BF)


def layer_three(rows, last_ref, hidden_ref):
    last = jnp.dot(last_ref[...], hidden_ref[...], preferred_element_type=F32)
    left, _ = shifted(last[0:rows])
    _, right = shifted(last[2 * rows : 3 * rows])
    return left + last[rows : 2 * rows] + right


def networks(entries, own, weights, scratch):
    one_ref, middle_ref, bias_ref, last_ref = weights
    taps, hidden = scratch[0:PLANES], scratch[PLANES : 2 * PLANES]
    for k in range(PLANES):
        layer_one(spread_entry(*entries[k]), own + 4, one_ref, taps[k])
    for k in range(PLANES):
        layer_two(own + 2, middle_ref, bias_ref, taps[k], hidden[k])
    return [layer_three(-(-own // 8) * 8, last_ref, hidden[k]) for k in range(PLANES)]


def network_scratch(own):
    return [pltpu.VMEM(((own + 4) * 192, 256), BF)] * PLANES + [
        pltpu.VMEM(((own + 2) * 64, 256), BF)
    ] * PLANES


def axial_kernel(
    subset_ref,
    timestep_ref,
    volume_ref,
    first_ref,
    second_ref,
    taps_in_ref,
    bias_in_ref,
    bias_mid_ref,
    taps_out_ref,
    taps_mid_ref,
    projector_ref,
    axial_ref,
    partial_ref,
    sent_ref,
    chosen_ref,
    picked_ref,
    sem,
    *scratch,
):
    copy = pltpu.make_async_copy(projector_ref.at[subset_ref[0] % SUBSETS], chosen_ref, sem)
    copy.start()
    weights, scratch = scratch[0:4], scratch[4:]
    raw = (taps_in_ref, bias_in_ref, bias_mid_ref, taps_out_ref, taps_mid_ref)
    build_from(AXIAL, lax.axis_index("gy"), 16, raw, weights)
    axial_ref[...] = jnp.zeros_like(axial_ref)
    scale_in, scale_out = noise_scales(timestep_ref)

    def planes(step, carry):
        entries = []
        for k in range(PLANES):
            p = step * PLANES + k
            entries.append((volume_ref[p] * scale_in, first_ref[p] * scale_in, second_ref[p] * scale_in))
        nets = networks(entries, 8, weights, scratch)
        for k in range(PLANES):
            p = step * PLANES + k
            value = volume_ref[p] + scale_out * nets[k]
            for y in range(8):
                axial_ref[y, pl.ds(p, 1), :] = value[y : y + 1, :]
        return carry

    lax.fori_loop(0, 12 // PLANES, planes, 0)
    copy.wait()
    flat = axial_ref[...].reshape(128, 256).astype(BF)
    lane = lax.broadcasted_iota(jnp.int32, (16, 256), 1) % 8
    for part in range(32):
        product = lax.dot_general(
            flat,
            chosen_ref[part * 256 : (part + 1) * 256, :],
            (((1,), (1,)), ((), ())),
            preferred_element_type=F32,
        )
        picked = product[0:16]
        for y in range(1, 8):
            picked = jnp.where(lane == y, product[y * 16 : (y + 1) * 16], picked)
        row, column = (part // 4) * 16, (part % 4) * 256
        picked_ref[row : row + 16, column : column + 256] = picked
    picked = picked_ref[...]
    high = picked.astype(BF)
    low = (picked - high.astype(F32)).astype(BF)
    fold = jnp.where(iota((1024, 128), 0) // 8 == iota((1024, 128), 1), 1.0, 0.0).astype(BF)
    partial = jnp.dot(high, fold, preferred_element_type=F32) + jnp.dot(
        low, fold, preferred_element_type=F32
    )
    partial_ref[...] = partial
    sent_ref[...] = partial.astype(BF)


def choose_kernel(subset_ref, _, projector_ref, chosen_ref, sem):
    copy = pltpu.make_async_copy(projector_ref.at[subset_ref[0] % SUBSETS], chosen_ref, sem)
    copy.start()
    copy.wait()


def back_kernel(
    subset_ref,
    measured_ref,
    sinogram_ref,
    axial_ref,
    chosen_ref,
    corrected_ref,
    residual_ref,
    held_ref,
):
    residual = measured_ref[...] - sinogram_ref[...]
    held_ref[...] = residual
    unfold = jnp.where(iota((128, 1024), 1) // 8 == iota((128, 1024), 0), 1.0, 0.0).astype(BF)
    wide = jnp.dot(residual.astype(BF), unfold, preferred_element_type=F32).astype(BF)
    lane = lax.broadcasted_iota(jnp.int32, (16, 1024), 1) % 8
    zero = jnp.zeros((), BF)
    total = jnp.zeros((128, 256), F32)
    for part in range(8):
        rays = wide[part * 16 : (part + 1) * 16]
        spread = jnp.concatenate([jnp.where(lane == y, rays, zero) for y in range(8)], axis=0)
        total = total + jnp.dot(
            spread, chosen_ref[part * 1024 : (part + 1) * 1024, :], preferred_element_type=F32
        )
    corrected_ref[...] = axial_ref[...] + (relaxation(subset_ref) * total).reshape(8, 16, 256)
    index = lax.axis_index("gy")
    block = held_ref[pl.ds(pl.multiple_of((index // 2) * 16, 16), 16), :]
    residual_ref[...] = jnp.where(index % 2 == 1, block[0:12, 64:128], block[0:12, 0:64])


def coronal_kernel(
    timestep_ref,
    corrected_ref,
    first_ref,
    second_ref,
    one_ref,
    middle_ref,
    bias_ref,
    last_ref,
    restored_ref,
    *scratch,
):
    scale_in, scale_out = noise_scales(timestep_ref)
    weights = (one_ref, middle_ref, bias_ref, last_ref)

    def planes(step, carry):
        entries = []
        for k in range(PLANES):
            p = step * PLANES + k
            entries.append((corrected_ref[p] * scale_in, first_ref[p] * scale_in, second_ref[p] * scale_in))
        nets = networks(entries, 12, weights, scratch)
        for k in range(PLANES):
            p = step * PLANES + k
            value = corrected_ref[p] + scale_out * nets[k]
            for z in range(12):
                restored_ref[z, pl.ds(p, 1), :] = value[z : z + 1, :]
        return carry

    lax.fori_loop(0, 8 // PLANES, planes, 0)


def vmem():
    return pl.BlockSpec(memory_space=pltpu.VMEM)


def hbm():
    return pl.BlockSpec(memory_space=pltpu.HBM)


def smem():
    return pl.BlockSpec(memory_space=pltpu.SMEM)


def params(limit):
    return pltpu.CompilerParams(vmem_limit_bytes=limit << 20)


def inner_pairs(size):
    return [(i, i ^ 1) for i in range(size)]


def outer_pairs(size):
    ups = [(i, i + 1) for i in range(1, size - 1, 2)]
    return ups + [(j, i) for i, j in ups]


def exchange(leading, trailing, axis, ordered):
    size = lax.axis_size(axis)
    odd = lax.axis_index(axis) % 2 == 1
    inner = jnp.where(odd, leading, trailing)
    outer = jnp.where(odd, trailing, leading)
    first = lax.ppermute(inner, axis, inner_pairs(size))
    if ordered:
        first, outer = lax.optimization_barrier((first, outer))
    second = lax.ppermute(outer, axis, outer_pairs(size))
    return first, second


def sum_over_gy(partial, sent, later):
    def partner(value, bits):
        return lax.ppermute(value, "gy", [(i, i ^ bits) for i in range(16)]).astype(F32)

    total = partial + partner(sent, 1)
    sent = total.astype(BF)
    total = total + partner(sent, 2) + partner(sent, 4) + partner(sent, 6)
    sent, later = lax.optimization_barrier((total.astype(BF), later))
    return total + partner(sent, 8), later, sent


def per_device(
    volume,
    projector,
    measured,
    subset,
    timestep,
    axial_in,
    axial_bias_in,
    axial_mid,
    axial_bias_mid,
    axial_out,
    coronal_in,
    coronal_bias_in,
    coronal_mid,
    coronal_bias_mid,
    coronal_out,
):
    first, second = exchange(volume[:, :HALO], volume[:, -HALO:], "gy", False)
    prepared = pl.pallas_call(
        prepare_kernel,
        name="prepare",
        out_shape=tuple(jax.ShapeDtypeStruct(*shape) for shape in weight_shapes(12))
        + (jax.ShapeDtypeStruct((128, 128), F32),),
        in_specs=[vmem()] * 6,
        out_specs=(vmem(),) * 5,
        compiler_params=params(40),
        cost_estimate=pl.CostEstimate(flops=1000000, bytes_accessed=3000000, transcendentals=0),
    )(
        coronal_in[:, :, 0],
        coronal_bias_in[None],
        coronal_bias_mid[None],
        coronal_out[:, 0, :],
        coronal_mid,
        measured.T,
    )
    coronal_weights, turned = prepared[0:4], prepared[4]
    flat_projector = projector.reshape(4, 8192, 256)
    axial, partial, sent = pl.pallas_call(
        axial_kernel,
        name="axial",
        out_shape=(
            jax.ShapeDtypeStruct((8, 16, 256), F32),
            jax.ShapeDtypeStruct((128, 128), F32),
            jax.ShapeDtypeStruct((128, 128), BF),
        ),
        in_specs=[smem()] * 2 + [vmem()] * 8 + [hbm()],
        out_specs=(vmem(),) * 3,
        scratch_shapes=[
            pltpu.VMEM((8192, 256), BF),
            pltpu.VMEM((128, 1024), F32),
            pltpu.SemaphoreType.DMA,
        ]
        + [pltpu.VMEM(*shape) for shape in weight_shapes(8)]
        + network_scratch(8),
        compiler_params=params(60),
    )(
        subset,
        timestep,
        volume,
        first,
        second,
        axial_in[:, :, 0],
        axial_bias_in[None],
        axial_bias_mid[None],
        axial_out[:, 0, :],
        axial_mid,
        flat_projector,
    )
    zero = timestep[0].astype(F32) * 0.0
    partial = lax.optimization_barrier(partial + zero)
    sinogram, axial, sent = sum_over_gy(partial, sent, axial)
    chosen = pl.pallas_call(
        choose_kernel,
        name="choose",
        out_shape=jax.ShapeDtypeStruct((8192, 256), BF),
        in_specs=[smem(), vmem(), hbm()],
        out_specs=vmem(),
        scratch_shapes=[pltpu.SemaphoreType.DMA],
        compiler_params=params(46),
        cost_estimate=pl.CostEstimate(flops=0, bytes_accessed=8 << 20, transcendentals=0),
    )(subset, sent, flat_projector)
    axial = lax.optimization_barrier(axial + zero)
    corrected, residual = pl.pallas_call(
        back_kernel,
        name="back",
        out_shape=(
            jax.ShapeDtypeStruct((8, 16, 256), F32),
            jax.ShapeDtypeStruct((12, 64), F32),
        ),
        in_specs=[smem()] + [vmem()] * 4,
        out_specs=(vmem(), vmem()),
        scratch_shapes=[pltpu.VMEM((128, 128), F32)],
        compiler_params=params(40),
    )(subset, turned, sinogram, axial, chosen)
    first, second = exchange(corrected[:, :HALO], corrected[:, 12 - HALO : 12], "gz", False)
    restored = pl.pallas_call(
        coronal_kernel,
        name="coronal",
        out_shape=jax.ShapeDtypeStruct((12, 8, 256), F32),
        in_specs=[smem()] + [vmem()] * 7,
        out_specs=vmem(),
        scratch_shapes=network_scratch(12),
        compiler_params=params(48),
    )(timestep, corrected, first, second, *coronal_weights)
    return (restored, residual.T)


def solution(mesh):
    in_specs = (
        P("gz", "gy", None),
        P(None, None, "gy", None),
        P(None, "gz"),
    ) + (P(),) * 12
    out_specs = (P("gz", "gy", None), P("gy", "gz"))
    return jax.shard_map(
        per_device, mesh=mesh, in_specs=in_specs, out_specs=out_specs, check_vma=False
    )
```

```python
import jax
import jax.numpy as jnp
from jax import lax
from jax.experimental import pallas as pl
from jax.experimental.pallas import tpu as pltpu
from jax.sharding import PartitionSpec as P

SUBSETS = 4
SIGMA_STEP = 0.002
RELAX_TOP = 4.0
HALO = 3
PLANES = 4
BF = jnp.bfloat16
F32 = jnp.float32
AXIAL = (8, 8, 11, 14, 16)
CORONAL = (12, 16, 19, 22, 24)


def noise_scales(timestep_ref):
    sigma = jnp.full((1, 256), timestep_ref[0], jnp.int32).astype(F32) * SIGMA_STEP
    scale_in = 1.0 / jnp.sqrt(1.0 + sigma * sigma)
    return (scale_in, sigma * scale_in)


def relaxation(subset_ref):
    epoch = jnp.full((1, 256), subset_ref[0] // SUBSETS, jnp.int32).astype(F32)
    return RELAX_TOP / (1.0 + epoch / 64.0)


def iota(shape, dim):
    return lax.broadcasted_iota(jnp.int32, shape, dim)


def last_rows(own):
    return -(-3 * (-(-own // 8) * 8) // 16) * 16


def build_weights(layout, index, count, first_taps, first_bias, middle_bias, last_taps, middle_taps_ref, outs):
    own, first, second, ones, slots = layout
    one_ref, middle_ref, bias_ref, last_ref = outs
    rows_one, rows_two = own + 4, own + 2
    total = count * own
    odd = index % 2 == 1
    before = jnp.where(odd, first, second)
    after = jnp.where(odd, second, first)

    def keep(row):
        place = index * own + row
        return jnp.where((place >= 0) & (place < total), 1.0, 0.0).astype(F32)

    def slot(row):
        if row < HALO:
            return before + row
        if row < own + HALO:
            return row - HALO
        return after + row - own - HALO

    rows = jnp.concatenate([first_taps, first_bias, middle_bias, jnp.zeros((5, 64), F32)], axis=0)
    high = rows.astype(BF)
    rest = rows - high.astype(F32)
    middle = rest.astype(BF)
    low = (rest - middle.astype(F32)).astype(BF)
    stack = jnp.concatenate([high, middle, low], axis=0)
    picks = jnp.where(iota((48, 11 * 128), 0) % 16 == iota((48, 11 * 128), 1) // 128, 1.0, 0.0)
    spread = lax.dot_general(
        stack, picks.astype(BF), (((0,), (0,)), ((), ())), preferred_element_type=F32
    )
    columns = [spread[:, k * 128 : (k + 1) * 128] for k in range(11)]
    bias_ref[:, 0:128] = columns[10]
    bias_ref[:, 128:256] = columns[10]
    bias_high = columns[9].astype(BF).astype(F32)
    bias_low = columns[9] - bias_high
    lane = iota((64, 128), 1)
    for row in range(rows_one):
        block = jnp.where(lane == slots + ones, bias_high, 0.0)
        block = jnp.where(lane == slots + ones + 1, bias_low, block)
        for a in range(3):
            for b in range(3):
                block = jnp.where(lane == b * slots + slot(row + a), columns[3 * a + b], block)
        one_ref[row * 64 : (row + 1) * 64, :] = (block * keep(row - 2)).astype(BF)
    padded = last_rows(own)
    band = -(-own // 8) * 8
    sublane = iota((padded, 64), 0)
    for row in range(rows_two):
        block = jnp.zeros((padded, 64), F32)
        for a in range(3):
            if 0 <= row - a < own:
                for b in range(3):
                    tap = last_taps[3 * a + b : 3 * a + b + 1, :]
                    block = jnp.where(sublane == b * band + row - a, tap, block)
        last_ref[:, row * 64 : (row + 1) * 64] = (block * keep(row - 1)).astype(BF)
    middle_ref[...] = jnp.zeros_like(middle_ref)
    for out in range(2):
        for a in range(3):
            for b in range(3):
                column = (out + a) * 192 + b * 64
                middle_ref[out * 64 : (out + 1) * 64, column : column + 64] = middle_taps_ref[3 * a + b]


def build_from(layout, index, count, raw, outs):
    first_taps, first_bias, middle_bias, last_taps, middle_taps_ref = raw
    build_weights(
        layout,
        index,
        count,
        first_taps[...].astype(F32),
        first_bias[...],
        middle_bias[...],
        last_taps[...].astype(F32),
        middle_taps_ref,
        outs,
    )


def prepare_kernel(*refs):
    raw, measured_ref, outs, turned_ref = refs[0:5], refs[5], refs[6:10], refs[10]
    build_from(CORONAL, lax.axis_index("gz"), 8, raw, outs)
    turned_ref[...] = jnp.zeros_like(turned_ref)
    for part in range(8):
        turned_ref[part * 16 : part * 16 + 12, :] = measured_ref[:, part * 128 : (part + 1) * 128]


def weight_shapes(own):
    return [
        (((own + 4) * 64, 128), BF),
        ((128, 768), BF),
        ((64, 256), F32),
        ((last_rows(own), (own + 2) * 64), BF),
    ]


def shifted(block):
    lane = lax.broadcasted_iota(jnp.int32, block.shape, 1)
    zero = jnp.zeros((), block.dtype)
    across = block.shape[1]
    left = jnp.where(lane == 0, zero, pltpu.roll(block, 1, 1))
    right = jnp.where(lane == across - 1, zero, pltpu.roll(block, across - 1, 1))
    return left, right


def spread_entry(own, first, second):
    rows = [own, first, second, jnp.ones((2, own.shape[1]), F32)]
    entry = jnp.concatenate(rows, axis=0)
    left, right = shifted(entry)
    return jnp.concatenate([left, entry, right], axis=0).astype(BF)


def layer_one(spread, rows, one_ref, taps_ref):
    depth = spread.shape[0]
    for row in rows:
        hidden = jnp.dot(
            one_ref[row * 64 : (row + 1) * 64, 0:depth], spread, preferred_element_type=F32
        )
        hidden = jnp.maximum(hidden, 0.0).astype(BF)
        left, right = shifted(hidden)
        taps_ref[row * 192 : row * 192 + 64, :] = left
        taps_ref[row * 192 + 64 : row * 192 + 128, :] = hidden
        taps_ref[row * 192 + 128 : row * 192 + 192, :] = right


def layer_two(pairs, middle_ref, bias_ref, taps_ref, hidden_ref, base=0):
    bias = bias_ref[...]
    for row in pairs:
        summed = jnp.dot(
            middle_ref[...], taps_ref[row * 192 : (row + 4) * 192, :], preferred_element_type=F32
        )
        for k in range(2):
            value = jnp.maximum(summed[k * 64 : (k + 1) * 64] + bias, 0.0)
            place = (row + k - base) * 64
            hidden_ref[place : place + 64, :] = value.astype(BF)


def layer_three(rows, last):
    left, _ = shifted(last[0:rows])
    _, right = shifted(last[2 * rows : 3 * rows])
    return left + last[rows : 2 * rows] + right


def networks(entries, own, weights, scratch):
    one_ref, middle_ref, bias_ref, last_ref = weights
    taps, hidden = scratch[0:PLANES], scratch[PLANES : 2 * PLANES]
    for k in range(PLANES):
        layer_one(spread_entry(*entries[k]), range(own + 4), one_ref, taps[k])
    for k in range(PLANES):
        layer_two(range(0, own + 2, 2), middle_ref, bias_ref, taps[k], hidden[k])
    last = [jnp.dot(last_ref[...], hidden[k][...], preferred_element_type=F32) for k in range(PLANES)]
    return [layer_three(-(-own // 8) * 8, last[k]) for k in range(PLANES)]


def network_scratch(own):
    return [pltpu.VMEM(((own + 4) * 192, 256), BF)] * PLANES + [
        pltpu.VMEM(((own + 2) * 64, 256), BF)
    ] * PLANES


def axial_kernel(
    subset_ref,
    timestep_ref,
    volume_ref,
    first_ref,
    second_ref,
    taps_in_ref,
    bias_in_ref,
    bias_mid_ref,
    taps_out_ref,
    taps_mid_ref,
    projector_ref,
    axial_ref,
    partial_ref,
    sent_ref,
    chosen_ref,
    picked_ref,
    sem,
    *scratch,
):
    copy = pltpu.make_async_copy(projector_ref.at[subset_ref[0] % SUBSETS], chosen_ref, sem)
    copy.start()
    weights, scratch = scratch[0:4], scratch[4:]
    raw = (taps_in_ref, bias_in_ref, bias_mid_ref, taps_out_ref, taps_mid_ref)
    build_from(AXIAL, lax.axis_index("gy"), 16, raw, weights)
    axial_ref[...] = jnp.zeros_like(axial_ref)
    scale_in, scale_out = noise_scales(timestep_ref)

    def planes(step, carry):
        entries = []
        for k in range(PLANES):
            p = step * PLANES + k
            entries.append((volume_ref[p] * scale_in, first_ref[p] * scale_in, second_ref[p] * scale_in))
        nets = networks(entries, 8, weights, scratch)
        for k in range(PLANES):
            p = step * PLANES + k
            value = volume_ref[p] + scale_out * nets[k]
            for y in range(8):
                axial_ref[y, pl.ds(p, 1), :] = value[y : y + 1, :]
        return carry

    lax.fori_loop(0, 12 // PLANES, planes, 0)
    copy.wait()
    flat = axial_ref[...].reshape(128, 256).astype(BF)
    lane = lax.broadcasted_iota(jnp.int32, (16, 256), 1) % 8
    for part in range(32):
        product = lax.dot_general(
            flat,
            chosen_ref[part * 256 : (part + 1) * 256, :],
            (((1,), (1,)), ((), ())),
            preferred_element_type=F32,
        )
        picked = product[0:16]
        for y in range(1, 8):
            picked = jnp.where(lane == y, product[y * 16 : (y + 1) * 16], picked)
        row, column = (part // 4) * 16, (part % 4) * 256
        picked_ref[row : row + 16, column : column + 256] = picked
    picked = picked_ref[...]
    high = picked.astype(BF)
    low = (picked - high.astype(F32)).astype(BF)
    fold = jnp.where(iota((1024, 128), 0) // 8 == iota((1024, 128), 1), 1.0, 0.0).astype(BF)
    partial = jnp.dot(high, fold, preferred_element_type=F32) + jnp.dot(
        low, fold, preferred_element_type=F32
    )
    partial_ref[...] = partial
    sent_ref[...] = partial.astype(BF)


def choose_kernel(subset_ref, _, projector_ref, chosen_ref, sem):
    copy = pltpu.make_async_copy(projector_ref.at[subset_ref[0] % SUBSETS], chosen_ref, sem)
    copy.start()
    copy.wait()


def back_kernel(
    subset_ref,
    measured_ref,
    sinogram_ref,
    axial_ref,
    chosen_ref,
    corrected_ref,
    residual_ref,
    held_ref,
):
    residual = measured_ref[...] - sinogram_ref[...]
    held_ref[...] = residual
    unfold = jnp.where(iota((128, 1024), 1) // 8 == iota((128, 1024), 0), 1.0, 0.0).astype(BF)
    wide = jnp.dot(residual.astype(BF), unfold, preferred_element_type=F32).astype(BF)
    lane = lax.broadcasted_iota(jnp.int32, (16, 1024), 1) % 8
    zero = jnp.zeros((), BF)
    total = jnp.zeros((128, 256), F32)
    for part in range(8):
        rays = wide[part * 16 : (part + 1) * 16]
        spread = jnp.concatenate([jnp.where(lane == y, rays, zero) for y in range(8)], axis=0)
        total = total + jnp.dot(
            spread, chosen_ref[part * 1024 : (part + 1) * 1024, :], preferred_element_type=F32
        )
    corrected_ref[...] = axial_ref[...] + (relaxation(subset_ref) * total).reshape(8, 16, 256)
    index = lax.axis_index("gy")
    block = held_ref[pl.ds(pl.multiple_of((index // 2) * 16, 16), 16), :]
    residual_ref[...] = jnp.where(index % 2 == 1, block[0:12, 64:128], block[0:12, 0:64])


def inner_kernel(
    timestep_ref, corrected_ref, one_ref, middle_ref, bias_ref, last_ref, inner_ref, *scratch
):
    taps, hidden = scratch[0:PLANES], scratch[PLANES:]
    scale_in, _ = noise_scales(timestep_ref)
    absent = jnp.zeros((HALO, 256), F32)

    def planes(step, carry):
        for k in range(PLANES):
            entry = corrected_ref[step * PLANES + k] * scale_in
            layer_one(spread_entry(entry, absent, absent), range(4, 12), one_ref, taps[k])
        for k in range(PLANES):
            layer_two((4, 6, 8), middle_ref, bias_ref, taps[k], hidden[k], 4)
        for k in range(PLANES):
            inner_ref[step * PLANES + k] = jnp.dot(
                last_ref[:, 256:640], hidden[k][...], preferred_element_type=F32
            )
        return carry

    lax.fori_loop(0, 8 // PLANES, planes, 0)


def coronal_kernel(
    timestep_ref,
    corrected_ref,
    first_ref,
    second_ref,
    inner_ref,
    one_ref,
    middle_ref,
    bias_ref,
    last_ref,
    restored_ref,
    *scratch,
):
    scale_in, scale_out = noise_scales(timestep_ref)
    taps, low, high = scratch[0:PLANES], scratch[PLANES : 2 * PLANES], scratch[2 * PLANES :]
    edges = (*range(0, 6), *range(10, 16))

    def planes(step, carry):
        for k in range(PLANES):
            p = step * PLANES + k
            rows = [ref[p] * scale_in for ref in (corrected_ref, first_ref, second_ref)]
            layer_one(spread_entry(*rows), edges, one_ref, taps[k])
        for k in range(PLANES):
            layer_two((0, 2), middle_ref, bias_ref, taps[k], low[k])
            layer_two((10, 12), middle_ref, bias_ref, taps[k], high[k], 10)
        for k in range(PLANES):
            p = step * PLANES + k
            last = inner_ref[p]
            last = last + jnp.dot(last_ref[:, 0:256], low[k][...], preferred_element_type=F32)
            last = last + jnp.dot(last_ref[:, 640:896], high[k][...], preferred_element_type=F32)
            value = corrected_ref[p] + scale_out * layer_three(16, last)
            for z in range(12):
                restored_ref[z, pl.ds(p, 1), :] = value[z : z + 1, :]
        return carry

    lax.fori_loop(0, 8 // PLANES, planes, 0)


def vmem():
    return pl.BlockSpec(memory_space=pltpu.VMEM)


def hbm():
    return pl.BlockSpec(memory_space=pltpu.HBM)


def smem():
    return pl.BlockSpec(memory_space=pltpu.SMEM)


def params(limit):
    return pltpu.CompilerParams(vmem_limit_bytes=limit << 20)


def inner_pairs(size):
    return [(i, i ^ 1) for i in range(size)]


def outer_pairs(size):
    ups = [(i, i + 1) for i in range(1, size - 1, 2)]
    return ups + [(j, i) for i, j in ups]


def exchange(leading, trailing, axis, ordered):
    size = lax.axis_size(axis)
    odd = lax.axis_index(axis) % 2 == 1
    inner = jnp.where(odd, leading, trailing)
    outer = jnp.where(odd, trailing, leading)
    first = lax.ppermute(inner, axis, inner_pairs(size))
    if ordered:
        first, outer = lax.optimization_barrier((first, outer))
    second = lax.ppermute(outer, axis, outer_pairs(size))
    return first, second


def sum_over_gy(partial, sent, later):
    def partner(value, bits):
        return lax.ppermute(value, "gy", [(i, i ^ bits) for i in range(16)]).astype(F32)

    total = partial + partner(sent, 1)
    sent = total.astype(BF)
    total = total + partner(sent, 2) + partner(sent, 4) + partner(sent, 6)
    sent, later = lax.optimization_barrier((total.astype(BF), later))
    return total + partner(sent, 8), later, sent


def per_device(
    volume,
    projector,
    measured,
    subset,
    timestep,
    axial_in,
    axial_bias_in,
    axial_mid,
    axial_bias_mid,
    axial_out,
    coronal_in,
    coronal_bias_in,
    coronal_mid,
    coronal_bias_mid,
    coronal_out,
):
    first, second = exchange(volume[:, :HALO], volume[:, -HALO:], "gy", False)
    prepared = pl.pallas_call(
        prepare_kernel,
        name="prepare",
        out_shape=tuple(jax.ShapeDtypeStruct(*shape) for shape in weight_shapes(12))
        + (jax.ShapeDtypeStruct((128, 128), F32),),
        in_specs=[vmem()] * 6,
        out_specs=(vmem(),) * 5,
        compiler_params=params(40),
        cost_estimate=pl.CostEstimate(flops=1000000, bytes_accessed=3000000, transcendentals=0),
    )(
        coronal_in[:, :, 0],
        coronal_bias_in[None],
        coronal_bias_mid[None],
        coronal_out[:, 0, :],
        coronal_mid,
        measured.T,
    )
    coronal_weights, turned = prepared[0:4], prepared[4]
    flat_projector = projector.reshape(4, 8192, 256)
    axial, partial, sent = pl.pallas_call(
        axial_kernel,
        name="axial",
        out_shape=(
            jax.ShapeDtypeStruct((8, 16, 256), F32),
            jax.ShapeDtypeStruct((128, 128), F32),
            jax.ShapeDtypeStruct((128, 128), BF),
        ),
        in_specs=[smem()] * 2 + [vmem()] * 8 + [hbm()],
        out_specs=(vmem(),) * 3,
        scratch_shapes=[
            pltpu.VMEM((8192, 256), BF),
            pltpu.VMEM((128, 1024), F32),
            pltpu.SemaphoreType.DMA,
        ]
        + [pltpu.VMEM(*shape) for shape in weight_shapes(8)]
        + network_scratch(8),
        compiler_params=params(60),
    )(
        subset,
        timestep,
        volume,
        first,
        second,
        axial_in[:, :, 0],
        axial_bias_in[None],
        axial_bias_mid[None],
        axial_out[:, 0, :],
        axial_mid,
        flat_projector,
    )
    zero = timestep[0].astype(F32) * 0.0
    partial = lax.optimization_barrier(partial + zero)
    sinogram, axial, sent = sum_over_gy(partial, sent, axial)
    chosen = pl.pallas_call(
        choose_kernel,
        name="choose",
        out_shape=jax.ShapeDtypeStruct((8192, 256), BF),
        in_specs=[smem(), vmem(), hbm()],
        out_specs=vmem(),
        scratch_shapes=[pltpu.SemaphoreType.DMA],
        compiler_params=params(46),
        cost_estimate=pl.CostEstimate(flops=0, bytes_accessed=8 << 20, transcendentals=0),
    )(subset, sent, flat_projector)
    axial = lax.optimization_barrier(axial + zero)
    corrected, residual = pl.pallas_call(
        back_kernel,
        name="back",
        out_shape=(
            jax.ShapeDtypeStruct((8, 16, 256), F32),
            jax.ShapeDtypeStruct((12, 64), F32),
        ),
        in_specs=[smem()] + [vmem()] * 4,
        out_specs=(vmem(), vmem()),
        scratch_shapes=[pltpu.VMEM((128, 128), F32)],
        compiler_params=params(40),
    )(subset, turned, sinogram, axial, chosen)
    first, second = exchange(corrected[:, :HALO], corrected[:, 12 - HALO : 12], "gz", False)
    taps_scratch = [pltpu.VMEM((16 * 192, 256), BF)] * PLANES
    inner = pl.pallas_call(
        inner_kernel,
        name="inner",
        out_shape=jax.ShapeDtypeStruct((8, 48, 256), F32),
        in_specs=[smem()] + [vmem()] * 5,
        out_specs=vmem(),
        scratch_shapes=taps_scratch + [pltpu.VMEM((6 * 64, 256), BF)] * PLANES,
        compiler_params=params(40),
        cost_estimate=pl.CostEstimate(flops=2000000000, bytes_accessed=2 << 20, transcendentals=0),
    )(timestep, corrected, *coronal_weights)
    restored = pl.pallas_call(
        coronal_kernel,
        name="coronal",
        out_shape=jax.ShapeDtypeStruct((12, 8, 256), F32),
        in_specs=[smem()] + [vmem()] * 8,
        out_specs=vmem(),
        scratch_shapes=taps_scratch + [pltpu.VMEM((256, 256), BF)] * (2 * PLANES),
        compiler_params=params(40),
    )(timestep, corrected, first, second, inner, *coronal_weights)
    return (restored, residual.T)


def solution(mesh):
    in_specs = (
        P("gz", "gy", None),
        P(None, None, "gy", None),
        P(None, "gz"),
    ) + (P(),) * 12
    out_specs = (P("gz", "gy", None), P("gy", "gz"))
    return jax.shard_map(
        per_device, mesh=mesh, in_specs=in_specs, out_specs=out_specs, check_vma=False
    )
```

```python
import jax
import jax.numpy as jnp
from jax import lax
from jax.experimental import pallas as pl
from jax.experimental.pallas import tpu as pltpu
from jax.sharding import PartitionSpec as P

SUBSETS = 4
SIGMA_STEP = 0.002
RELAX_TOP = 4.0
HALO = 3
AXIAL_PLANES = 6
CORONAL_PLANES = 8
BF = jnp.bfloat16
F32 = jnp.float32
AXIAL = (8, 8, 11, 14, 16)
CORONAL = (12, 16, 19, 22, 24)


def noise_scales(timestep_ref):
    sigma = jnp.full((1, 256), timestep_ref[0], jnp.int32).astype(F32) * SIGMA_STEP
    scale_in = 1.0 / jnp.sqrt(1.0 + sigma * sigma)
    return (scale_in, sigma * scale_in)


def relaxation(subset_ref):
    epoch = jnp.full((1, 256), subset_ref[0] // SUBSETS, jnp.int32).astype(F32)
    return RELAX_TOP / (1.0 + epoch / 64.0)


def iota(shape, dim):
    return lax.broadcasted_iota(jnp.int32, shape, dim)


def last_rows(own):
    return -(-3 * (-(-own // 8) * 8) // 16) * 16


def build_weights(layout, index, count, first_taps, first_bias, middle_bias, last_taps, middle_taps_ref, outs):
    own, first, second, ones, slots = layout
    one_ref, middle_ref, bias_ref, last_ref = outs
    rows_one, rows_two = own + 4, own + 2
    total = count * own
    odd = index % 2 == 1
    before = jnp.where(odd, first, second)
    after = jnp.where(odd, second, first)

    def keep(row):
        place = index * own + row
        return jnp.where((place >= 0) & (place < total), 1.0, 0.0).astype(F32)

    def slot(row):
        if row < HALO:
            return before + row
        if row < own + HALO:
            return row - HALO
        return after + row - own - HALO

    rows = jnp.concatenate([first_taps, first_bias, middle_bias, jnp.zeros((5, 64), F32)], axis=0)
    high = rows.astype(BF)
    rest = rows - high.astype(F32)
    middle = rest.astype(BF)
    low = (rest - middle.astype(F32)).astype(BF)
    stack = jnp.concatenate([high, middle, low], axis=0)
    picks = jnp.where(iota((48, 11 * 128), 0) % 16 == iota((48, 11 * 128), 1) // 128, 1.0, 0.0)
    spread = lax.dot_general(
        stack, picks.astype(BF), (((0,), (0,)), ((), ())), preferred_element_type=F32
    )
    columns = [spread[:, k * 128 : (k + 1) * 128] for k in range(11)]
    bias_ref[:, 0:128] = columns[10]
    bias_ref[:, 128:256] = columns[10]
    bias_high = columns[9].astype(BF).astype(F32)
    bias_low = columns[9] - bias_high
    lane = iota((64, 128), 1)
    for row in range(rows_one):
        block = jnp.where(lane == slots + ones, bias_high, 0.0)
        block = jnp.where(lane == slots + ones + 1, bias_low, block)
        for a in range(3):
            for b in range(3):
                block = jnp.where(lane == b * slots + slot(row + a), columns[3 * a + b], block)
        one_ref[row * 64 : (row + 1) * 64, :] = (block * keep(row - 2)).astype(BF)
    padded = last_rows(own)
    band = -(-own // 8) * 8
    sublane = iota((padded, 64), 0)
    for row in range(rows_two):
        block = jnp.zeros((padded, 64), F32)
        for a in range(3):
            if 0 <= row - a < own:
                for b in range(3):
                    tap = last_taps[3 * a + b : 3 * a + b + 1, :]
                    block = jnp.where(sublane == b * band + row - a, tap, block)
        last_ref[:, row * 64 : (row + 1) * 64] = (block * keep(row - 1)).astype(BF)
    middle_ref[...] = jnp.zeros_like(middle_ref)
    for out in range(2):
        for a in range(3):
            for b in range(3):
                column = (out + a) * 192 + b * 64
                middle_ref[out * 64 : (out + 1) * 64, column : column + 64] = middle_taps_ref[3 * a + b]


def build_from(layout, index, count, raw, outs):
    first_taps, first_bias, middle_bias, last_taps, middle_taps_ref = raw
    build_weights(
        layout,
        index,
        count,
        first_taps[...].astype(F32),
        first_bias[...],
        middle_bias[...],
        last_taps[...].astype(F32),
        middle_taps_ref,
        outs,
    )


def prepare_kernel(*refs):
    raw, measured_ref, outs, turned_ref = refs[0:5], refs[5], refs[6:10], refs[10]
    build_from(CORONAL, lax.axis_index("gz"), 8, raw, outs)
    turned_ref[...] = jnp.zeros_like(turned_ref)
    for part in range(8):
        turned_ref[part * 16 : part * 16 + 12, :] = measured_ref[:, part * 128 : (part + 1) * 128]


def weight_shapes(own):
    return [
        (((own + 4) * 64, 128), BF),
        ((128, 768), BF),
        ((64, 256), F32),
        ((last_rows(own), (own + 2) * 64), BF),
    ]


def shifted(block):
    lane = lax.broadcasted_iota(jnp.int32, block.shape, 1)
    zero = jnp.zeros((), block.dtype)
    across = block.shape[1]
    left = jnp.where(lane == 0, zero, pltpu.roll(block, 1, 1))
    right = jnp.where(lane == across - 1, zero, pltpu.roll(block, across - 1, 1))
    return left, right


def spread_entry(own, first, second):
    rows = [own, first, second, jnp.ones((2, own.shape[1]), F32)]
    entry = jnp.concatenate(rows, axis=0)
    left, right = shifted(entry)
    return jnp.concatenate([left, entry, right], axis=0).astype(BF)


def layer_one(spread, rows, one_ref, taps_ref):
    depth = spread.shape[0]
    for row in rows:
        hidden = jnp.dot(
            one_ref[row * 64 : (row + 1) * 64, 0:depth], spread, preferred_element_type=F32
        )
        hidden = jnp.maximum(hidden, 0.0).astype(BF)
        left, right = shifted(hidden)
        taps_ref[row * 192 : row * 192 + 64, :] = left
        taps_ref[row * 192 + 64 : row * 192 + 128, :] = hidden
        taps_ref[row * 192 + 128 : row * 192 + 192, :] = right


def layer_two(pairs, middle_ref, bias_ref, taps_ref, hidden_ref, base=0):
    bias = bias_ref[...]
    for row in pairs:
        summed = jnp.dot(
            middle_ref[...], taps_ref[row * 192 : (row + 4) * 192, :], preferred_element_type=F32
        )
        for k in range(2):
            value = jnp.maximum(summed[k * 64 : (k + 1) * 64] + bias, 0.0)
            place = (row + k - base) * 64
            hidden_ref[place : place + 64, :] = value.astype(BF)


def layer_three(rows, last):
    left, _ = shifted(last[0:rows])
    _, right = shifted(last[2 * rows : 3 * rows])
    return left + last[rows : 2 * rows] + right


def networks(entries, own, weights, scratch):
    one_ref, middle_ref, bias_ref, last_ref = weights
    taps, hidden = scratch[0:AXIAL_PLANES], scratch[AXIAL_PLANES : 2 * AXIAL_PLANES]
    for k in range(AXIAL_PLANES):
        layer_one(spread_entry(*entries[k]), range(own + 4), one_ref, taps[k])
    for k in range(AXIAL_PLANES):
        layer_two(range(0, own + 2, 2), middle_ref, bias_ref, taps[k], hidden[k])
    last = [jnp.dot(last_ref[...], hidden[k][...], preferred_element_type=F32) for k in range(AXIAL_PLANES)]
    return [layer_three(-(-own // 8) * 8, last[k]) for k in range(AXIAL_PLANES)]


def network_scratch(own):
    return [pltpu.VMEM(((own + 4) * 192, 256), BF)] * AXIAL_PLANES + [
        pltpu.VMEM(((own + 2) * 64, 256), BF)
    ] * AXIAL_PLANES


def axial_kernel(
    subset_ref,
    timestep_ref,
    volume_ref,
    first_ref,
    second_ref,
    taps_in_ref,
    bias_in_ref,
    bias_mid_ref,
    taps_out_ref,
    taps_mid_ref,
    projector_ref,
    axial_ref,
    partial_ref,
    sent_ref,
    chosen_ref,
    picked_ref,
    sem,
    *scratch,
):
    copy = pltpu.make_async_copy(projector_ref.at[subset_ref[0] % SUBSETS], chosen_ref, sem)
    copy.start()
    weights, scratch = scratch[0:4], scratch[4:]
    raw = (taps_in_ref, bias_in_ref, bias_mid_ref, taps_out_ref, taps_mid_ref)
    build_from(AXIAL, lax.axis_index("gy"), 16, raw, weights)
    axial_ref[...] = jnp.zeros_like(axial_ref)
    scale_in, scale_out = noise_scales(timestep_ref)

    def planes(step, carry):
        entries = []
        for k in range(AXIAL_PLANES):
            p = step * AXIAL_PLANES + k
            entries.append((volume_ref[p] * scale_in, first_ref[p] * scale_in, second_ref[p] * scale_in))
        nets = networks(entries, 8, weights, scratch)
        for k in range(AXIAL_PLANES):
            p = step * AXIAL_PLANES + k
            value = volume_ref[p] + scale_out * nets[k]
            for y in range(8):
                axial_ref[y, pl.ds(p, 1), :] = value[y : y + 1, :]
        return carry

    lax.fori_loop(0, 12 // AXIAL_PLANES, planes, 0)
    copy.wait()
    flat = axial_ref[...].reshape(128, 256).astype(BF)
    lane = lax.broadcasted_iota(jnp.int32, (16, 256), 1) % 8
    for part in range(32):
        product = lax.dot_general(
            flat,
            chosen_ref[part * 256 : (part + 1) * 256, :],
            (((1,), (1,)), ((), ())),
            preferred_element_type=F32,
        )
        picked = product[0:16]
        for y in range(1, 8):
            picked = jnp.where(lane == y, product[y * 16 : (y + 1) * 16], picked)
        row, column = (part // 4) * 16, (part % 4) * 256
        picked_ref[row : row + 16, column : column + 256] = picked
    picked = picked_ref[...]
    high = picked.astype(BF)
    low = (picked - high.astype(F32)).astype(BF)
    fold = jnp.where(iota((1024, 128), 0) // 8 == iota((1024, 128), 1), 1.0, 0.0).astype(BF)
    partial = jnp.dot(high, fold, preferred_element_type=F32) + jnp.dot(
        low, fold, preferred_element_type=F32
    )
    partial_ref[...] = partial
    sent_ref[...] = partial.astype(BF)


def choose_kernel(subset_ref, _, projector_ref, chosen_ref, sem):
    copy = pltpu.make_async_copy(projector_ref.at[subset_ref[0] % SUBSETS], chosen_ref, sem)
    copy.start()
    copy.wait()


def back_kernel(
    subset_ref,
    measured_ref,
    sinogram_ref,
    axial_ref,
    chosen_ref,
    corrected_ref,
    residual_ref,
    held_ref,
):
    residual = measured_ref[...] - sinogram_ref[...]
    held_ref[...] = residual
    unfold = jnp.where(iota((128, 1024), 1) // 8 == iota((128, 1024), 0), 1.0, 0.0).astype(BF)
    wide = jnp.dot(residual.astype(BF), unfold, preferred_element_type=F32).astype(BF)
    lane = lax.broadcasted_iota(jnp.int32, (16, 1024), 1) % 8
    zero = jnp.zeros((), BF)
    total = jnp.zeros((128, 256), F32)
    for part in range(8):
        rays = wide[part * 16 : (part + 1) * 16]
        spread = jnp.concatenate([jnp.where(lane == y, rays, zero) for y in range(8)], axis=0)
        total = total + jnp.dot(
            spread, chosen_ref[part * 1024 : (part + 1) * 1024, :], preferred_element_type=F32
        )
    corrected_ref[...] = axial_ref[...] + (relaxation(subset_ref) * total).reshape(8, 16, 256)
    index = lax.axis_index("gy")
    block = held_ref[pl.ds(pl.multiple_of((index // 2) * 16, 16), 16), :]
    residual_ref[...] = jnp.where(index % 2 == 1, block[0:12, 64:128], block[0:12, 0:64])


def inner_kernel(
    timestep_ref, corrected_ref, one_ref, middle_ref, bias_ref, last_ref, inner_ref, *scratch
):
    taps, hidden = scratch[0:CORONAL_PLANES], scratch[CORONAL_PLANES:]
    scale_in, _ = noise_scales(timestep_ref)
    absent = jnp.zeros((HALO, 256), F32)

    def planes(step, carry):
        for k in range(CORONAL_PLANES):
            entry = corrected_ref[step * CORONAL_PLANES + k] * scale_in
            layer_one(spread_entry(entry, absent, absent), range(4, 12), one_ref, taps[k])
        for k in range(CORONAL_PLANES):
            layer_two((4, 6, 8), middle_ref, bias_ref, taps[k], hidden[k], 4)
        for k in range(CORONAL_PLANES):
            inner_ref[step * CORONAL_PLANES + k] = jnp.dot(
                last_ref[:, 256:640], hidden[k][...], preferred_element_type=F32
            )
        return carry

    lax.fori_loop(0, 8 // CORONAL_PLANES, planes, 0)


def coronal_kernel(
    timestep_ref,
    corrected_ref,
    first_ref,
    second_ref,
    inner_ref,
    one_ref,
    middle_ref,
    bias_ref,
    last_ref,
    restored_ref,
    *scratch,
):
    scale_in, scale_out = noise_scales(timestep_ref)
    taps, low, high = scratch[0:CORONAL_PLANES], scratch[CORONAL_PLANES : 2 * CORONAL_PLANES], scratch[2 * CORONAL_PLANES :]
    edges = (*range(0, 6), *range(10, 16))

    def planes(step, carry):
        for k in range(CORONAL_PLANES):
            p = step * CORONAL_PLANES + k
            rows = [ref[p] * scale_in for ref in (corrected_ref, first_ref, second_ref)]
            layer_one(spread_entry(*rows), edges, one_ref, taps[k])
        for k in range(CORONAL_PLANES):
            layer_two((0, 2), middle_ref, bias_ref, taps[k], low[k])
            layer_two((10, 12), middle_ref, bias_ref, taps[k], high[k], 10)
        for k in range(CORONAL_PLANES):
            p = step * CORONAL_PLANES + k
            last = inner_ref[p]
            last = last + jnp.dot(last_ref[:, 0:256], low[k][...], preferred_element_type=F32)
            last = last + jnp.dot(last_ref[:, 640:896], high[k][...], preferred_element_type=F32)
            value = corrected_ref[p] + scale_out * layer_three(16, last)
            for z in range(12):
                restored_ref[z, pl.ds(p, 1), :] = value[z : z + 1, :]
        return carry

    lax.fori_loop(0, 8 // CORONAL_PLANES, planes, 0)


def vmem():
    return pl.BlockSpec(memory_space=pltpu.VMEM)


def hbm():
    return pl.BlockSpec(memory_space=pltpu.HBM)


def smem():
    return pl.BlockSpec(memory_space=pltpu.SMEM)


def params(limit):
    return pltpu.CompilerParams(vmem_limit_bytes=limit << 20)


def inner_pairs(size):
    return [(i, i ^ 1) for i in range(size)]


def outer_pairs(size):
    ups = [(i, i + 1) for i in range(1, size - 1, 2)]
    return ups + [(j, i) for i, j in ups]


def exchange(leading, trailing, axis, ordered):
    size = lax.axis_size(axis)
    odd = lax.axis_index(axis) % 2 == 1
    inner = jnp.where(odd, leading, trailing)
    outer = jnp.where(odd, trailing, leading)
    first = lax.ppermute(inner, axis, inner_pairs(size))
    if ordered:
        first, outer = lax.optimization_barrier((first, outer))
    second = lax.ppermute(outer, axis, outer_pairs(size))
    return first, second


def sum_over_gy(partial, sent, later):
    def partner(value, bits):
        return lax.ppermute(value, "gy", [(i, i ^ bits) for i in range(16)]).astype(F32)

    total = partial + partner(sent, 1)
    sent = total.astype(BF)
    total = total + partner(sent, 2) + partner(sent, 4) + partner(sent, 6)
    sent, later = lax.optimization_barrier((total.astype(BF), later))
    return total + partner(sent, 8), later, sent


def per_device(
    volume,
    projector,
    measured,
    subset,
    timestep,
    axial_in,
    axial_bias_in,
    axial_mid,
    axial_bias_mid,
    axial_out,
    coronal_in,
    coronal_bias_in,
    coronal_mid,
    coronal_bias_mid,
    coronal_out,
):
    first, second = exchange(volume[:, :HALO], volume[:, -HALO:], "gy", False)
    prepared = pl.pallas_call(
        prepare_kernel,
        name="prepare",
        out_shape=tuple(jax.ShapeDtypeStruct(*shape) for shape in weight_shapes(12))
        + (jax.ShapeDtypeStruct((128, 128), F32),),
        in_specs=[vmem()] * 6,
        out_specs=(vmem(),) * 5,
        compiler_params=params(40),
        cost_estimate=pl.CostEstimate(flops=1000000, bytes_accessed=3000000, transcendentals=0),
    )(
        coronal_in[:, :, 0],
        coronal_bias_in[None],
        coronal_bias_mid[None],
        coronal_out[:, 0, :],
        coronal_mid,
        measured.T,
    )
    coronal_weights, turned = prepared[0:4], prepared[4]
    flat_projector = projector.reshape(4, 8192, 256)
    axial, partial, sent = pl.pallas_call(
        axial_kernel,
        name="axial",
        out_shape=(
            jax.ShapeDtypeStruct((8, 16, 256), F32),
            jax.ShapeDtypeStruct((128, 128), F32),
            jax.ShapeDtypeStruct((128, 128), BF),
        ),
        in_specs=[smem()] * 2 + [vmem()] * 8 + [hbm()],
        out_specs=(vmem(),) * 3,
        scratch_shapes=[
            pltpu.VMEM((8192, 256), BF),
            pltpu.VMEM((128, 1024), F32),
            pltpu.SemaphoreType.DMA,
        ]
        + [pltpu.VMEM(*shape) for shape in weight_shapes(8)]
        + network_scratch(8),
        compiler_params=params(60),
    )(
        subset,
        timestep,
        volume,
        first,
        second,
        axial_in[:, :, 0],
        axial_bias_in[None],
        axial_bias_mid[None],
        axial_out[:, 0, :],
        axial_mid,
        flat_projector,
    )
    zero = timestep[0].astype(F32) * 0.0
    partial = lax.optimization_barrier(partial + zero)
    sinogram, axial, sent = sum_over_gy(partial, sent, axial)
    chosen = pl.pallas_call(
        choose_kernel,
        name="choose",
        out_shape=jax.ShapeDtypeStruct((8192, 256), BF),
        in_specs=[smem(), vmem(), hbm()],
        out_specs=vmem(),
        scratch_shapes=[pltpu.SemaphoreType.DMA],
        compiler_params=params(46),
        cost_estimate=pl.CostEstimate(flops=0, bytes_accessed=8 << 20, transcendentals=0),
    )(subset, sent, flat_projector)
    axial = lax.optimization_barrier(axial + zero)
    corrected, residual = pl.pallas_call(
        back_kernel,
        name="back",
        out_shape=(
            jax.ShapeDtypeStruct((8, 16, 256), F32),
            jax.ShapeDtypeStruct((12, 64), F32),
        ),
        in_specs=[smem()] + [vmem()] * 4,
        out_specs=(vmem(), vmem()),
        scratch_shapes=[pltpu.VMEM((128, 128), F32)],
        compiler_params=params(40),
    )(subset, turned, sinogram, axial, chosen)
    first, second = exchange(corrected[:, :HALO], corrected[:, 12 - HALO : 12], "gz", False)
    taps_scratch = [pltpu.VMEM((16 * 192, 256), BF)] * CORONAL_PLANES
    inner = pl.pallas_call(
        inner_kernel,
        name="inner",
        out_shape=jax.ShapeDtypeStruct((8, 48, 256), F32),
        in_specs=[smem()] + [vmem()] * 5,
        out_specs=vmem(),
        scratch_shapes=taps_scratch + [pltpu.VMEM((6 * 64, 256), BF)] * CORONAL_PLANES,
        compiler_params=params(40),
        cost_estimate=pl.CostEstimate(flops=2000000000, bytes_accessed=2 << 20, transcendentals=0),
    )(timestep, corrected, *coronal_weights)
    restored = pl.pallas_call(
        coronal_kernel,
        name="coronal",
        out_shape=jax.ShapeDtypeStruct((12, 8, 256), F32),
        in_specs=[smem()] + [vmem()] * 8,
        out_specs=vmem(),
        scratch_shapes=taps_scratch + [pltpu.VMEM((256, 256), BF)] * (2 * CORONAL_PLANES),
        compiler_params=params(40),
    )(timestep, corrected, first, second, inner, *coronal_weights)
    return (restored, residual.T)


def solution(mesh):
    in_specs = (
        P("gz", "gy", None),
        P(None, None, "gy", None),
        P(None, "gz"),
    ) + (P(),) * 12
    out_specs = (P("gz", "gy", None), P("gy", "gz"))
    return jax.shard_map(
        per_device, mesh=mesh, in_specs=in_specs, out_specs=out_specs, check_vma=False
    )
```

```python
import jax
import jax.numpy as jnp
from jax import lax
from jax.experimental import pallas as pl
from jax.experimental.pallas import tpu as pltpu
from jax.sharding import PartitionSpec as P

SUBSETS = 4
SIGMA_STEP = 0.002
RELAX_TOP = 4.0
HALO = 3
AXIAL_PLANES = 6
CORONAL_PLANES = 8
BF = jnp.bfloat16
F32 = jnp.float32
AXIAL = (8, 8, 11, 14, 16)
CORONAL = (12, 16, 19, 22, 24)


def noise_scales(timestep_ref):
    sigma = jnp.full((1, 256), timestep_ref[0], jnp.int32).astype(F32) * SIGMA_STEP
    scale_in = 1.0 / jnp.sqrt(1.0 + sigma * sigma)
    return (scale_in, sigma * scale_in)


def relaxation(subset_ref):
    epoch = jnp.full((1, 256), subset_ref[0] // SUBSETS, jnp.int32).astype(F32)
    return RELAX_TOP / (1.0 + epoch / 64.0)


def iota(shape, dim):
    return lax.broadcasted_iota(jnp.int32, shape, dim)


def last_rows(own):
    return -(-3 * (-(-own // 8) * 8) // 16) * 16


def build_weights(layout, index, count, first_taps, first_bias, middle_bias, last_taps, middle_taps_ref, outs):
    own, first, second, ones, slots = layout
    one_ref, middle_ref, bias_ref, last_ref = outs
    rows_one, rows_two = own + 4, own + 2
    total = count * own
    odd = index % 2 == 1
    before = jnp.where(odd, first, second)
    after = jnp.where(odd, second, first)

    def keep(row):
        place = index * own + row
        return jnp.where((place >= 0) & (place < total), 1.0, 0.0).astype(F32)

    def slot(row):
        if row < HALO:
            return before + row
        if row < own + HALO:
            return row - HALO
        return after + row - own - HALO

    rows = jnp.concatenate([first_taps, first_bias, middle_bias, jnp.zeros((5, 64), F32)], axis=0)
    high = rows.astype(BF)
    rest = rows - high.astype(F32)
    middle = rest.astype(BF)
    low = (rest - middle.astype(F32)).astype(BF)
    stack = jnp.concatenate([high, middle, low], axis=0)
    picks = jnp.where(iota((48, 11 * 128), 0) % 16 == iota((48, 11 * 128), 1) // 128, 1.0, 0.0)
    spread = lax.dot_general(
        stack, picks.astype(BF), (((0,), (0,)), ((), ())), preferred_element_type=F32
    )
    columns = [spread[:, k * 128 : (k + 1) * 128] for k in range(11)]
    bias_ref[:, 0:128] = columns[10]
    bias_ref[:, 128:256] = columns[10]
    bias_high = columns[9].astype(BF).astype(F32)
    bias_low = columns[9] - bias_high
    lane = iota((64, 128), 1)
    for row in range(rows_one):
        block = jnp.where(lane == slots + ones, bias_high, 0.0)
        block = jnp.where(lane == slots + ones + 1, bias_low, block)
        for a in range(3):
            for b in range(3):
                block = jnp.where(lane == b * slots + slot(row + a), columns[3 * a + b], block)
        one_ref[row * 64 : (row + 1) * 64, :] = (block * keep(row - 2)).astype(BF)
    padded = last_rows(own)
    band = -(-own // 8) * 8
    sublane = iota((padded, 64), 0)
    for row in range(rows_two):
        block = jnp.zeros((padded, 64), F32)
        for a in range(3):
            if 0 <= row - a < own:
                for b in range(3):
                    tap = last_taps[3 * a + b : 3 * a + b + 1, :]
                    block = jnp.where(sublane == b * band + row - a, tap, block)
        last_ref[:, row * 64 : (row + 1) * 64] = (block * keep(row - 1)).astype(BF)
    middle_ref[...] = jnp.zeros_like(middle_ref)
    for out in range(2):
        for a in range(3):
            for b in range(3):
                column = (out + a) * 192 + b * 64
                middle_ref[out * 64 : (out + 1) * 64, column : column + 64] = middle_taps_ref[3 * a + b]


def build_from(layout, index, count, raw, outs):
    first_taps, first_bias, middle_bias, last_taps, middle_taps_ref = raw
    build_weights(
        layout,
        index,
        count,
        first_taps[...].astype(F32),
        first_bias[...],
        middle_bias[...],
        last_taps[...].astype(F32),
        middle_taps_ref,
        outs,
    )


def prepare_kernel(*refs):
    raw, measured_ref, outs, turned_ref = refs[0:5], refs[5], refs[6:10], refs[10]
    build_from(CORONAL, lax.axis_index("gz"), 8, raw, outs)
    turned_ref[...] = jnp.zeros_like(turned_ref)
    for part in range(8):
        turned_ref[part * 16 : part * 16 + 12, :] = measured_ref[:, part * 128 : (part + 1) * 128]


def weight_shapes(own):
    return [
        (((own + 4) * 64, 128), BF),
        ((128, 768), BF),
        ((64, 256), F32),
        ((last_rows(own), (own + 2) * 64), BF),
    ]


def shifted(block):
    lane = lax.broadcasted_iota(jnp.int32, block.shape, 1)
    zero = jnp.zeros((), block.dtype)
    across = block.shape[1]
    left = jnp.where(lane == 0, zero, pltpu.roll(block, 1, 1))
    right = jnp.where(lane == across - 1, zero, pltpu.roll(block, across - 1, 1))
    return left, right


def spread_entry(own, first, second):
    rows = [own, first, second, jnp.ones((2, own.shape[1]), F32)]
    entry = jnp.concatenate(rows, axis=0)
    left, right = shifted(entry)
    return jnp.concatenate([left, entry, right], axis=0).astype(BF)


def layer_one(spread, rows, one_ref, taps_ref):
    depth = spread.shape[0]
    for row in rows:
        hidden = jnp.dot(
            one_ref[row * 64 : (row + 1) * 64, 0:depth], spread, preferred_element_type=F32
        )
        hidden = jnp.maximum(hidden, 0.0).astype(BF)
        left, right = shifted(hidden)
        taps_ref[row * 192 : row * 192 + 64, :] = left
        taps_ref[row * 192 + 64 : row * 192 + 128, :] = hidden
        taps_ref[row * 192 + 128 : row * 192 + 192, :] = right


def layer_two(pairs, middle_ref, bias_ref, taps_ref, hidden_ref, base=0):
    bias = bias_ref[...]
    for row in pairs:
        summed = jnp.dot(
            middle_ref[...], taps_ref[row * 192 : (row + 4) * 192, :], preferred_element_type=F32
        )
        for k in range(2):
            value = jnp.maximum(summed[k * 64 : (k + 1) * 64] + bias, 0.0)
            place = (row + k - base) * 64
            hidden_ref[place : place + 64, :] = value.astype(BF)


def layer_three(rows, last):
    left, _ = shifted(last[0:rows])
    _, right = shifted(last[2 * rows : 3 * rows])
    return left + last[rows : 2 * rows] + right


def networks(entries, own, weights, scratch):
    one_ref, middle_ref, bias_ref, last_ref = weights
    taps, hidden = scratch[0:AXIAL_PLANES], scratch[AXIAL_PLANES : 2 * AXIAL_PLANES]
    for k in range(AXIAL_PLANES):
        layer_one(spread_entry(*entries[k]), range(own + 4), one_ref, taps[k])
    for k in range(AXIAL_PLANES):
        layer_two(range(0, own + 2, 2), middle_ref, bias_ref, taps[k], hidden[k])
    last = [jnp.dot(last_ref[...], hidden[k][...], preferred_element_type=F32) for k in range(AXIAL_PLANES)]
    return [layer_three(-(-own // 8) * 8, last[k]) for k in range(AXIAL_PLANES)]


def network_scratch(own):
    return [pltpu.VMEM(((own + 4) * 192, 256), BF)] * AXIAL_PLANES + [
        pltpu.VMEM(((own + 2) * 64, 256), BF)
    ] * AXIAL_PLANES


def axial_kernel(
    subset_ref,
    timestep_ref,
    volume_ref,
    first_ref,
    second_ref,
    taps_in_ref,
    bias_in_ref,
    bias_mid_ref,
    taps_out_ref,
    taps_mid_ref,
    projector_ref,
    axial_ref,
    partial_ref,
    sent_ref,
    chosen_ref,
    picked_ref,
    sem,
    *scratch,
):
    copy = pltpu.make_async_copy(projector_ref.at[subset_ref[0] % SUBSETS], chosen_ref, sem)
    copy.start()
    weights, scratch = scratch[0:4], scratch[4:]
    raw = (taps_in_ref, bias_in_ref, bias_mid_ref, taps_out_ref, taps_mid_ref)
    build_from(AXIAL, lax.axis_index("gy"), 16, raw, weights)
    axial_ref[...] = jnp.zeros_like(axial_ref)
    scale_in, scale_out = noise_scales(timestep_ref)

    def planes(step, carry):
        entries = []
        for k in range(AXIAL_PLANES):
            p = step * AXIAL_PLANES + k
            entries.append((volume_ref[p] * scale_in, first_ref[p] * scale_in, second_ref[p] * scale_in))
        nets = networks(entries, 8, weights, scratch)
        for k in range(AXIAL_PLANES):
            p = step * AXIAL_PLANES + k
            value = volume_ref[p] + scale_out * nets[k]
            for y in range(8):
                axial_ref[y, pl.ds(p, 1), :] = value[y : y + 1, :]
        return carry

    lax.fori_loop(0, 12 // AXIAL_PLANES, planes, 0)
    copy.wait()
    flat = axial_ref[...].reshape(128, 256).astype(BF)
    lane = lax.broadcasted_iota(jnp.int32, (16, 256), 1) % 8
    for part in range(32):
        product = lax.dot_general(
            flat,
            chosen_ref[part * 256 : (part + 1) * 256, :],
            (((1,), (1,)), ((), ())),
            preferred_element_type=F32,
        )
        picked = product[0:16]
        for y in range(1, 8):
            picked = jnp.where(lane == y, product[y * 16 : (y + 1) * 16], picked)
        row, column = (part // 4) * 16, (part % 4) * 256
        picked_ref[row : row + 16, column : column + 256] = picked
    picked = picked_ref[...]
    high = picked.astype(BF)
    low = (picked - high.astype(F32)).astype(BF)
    fold = jnp.where(iota((1024, 128), 0) // 8 == iota((1024, 128), 1), 1.0, 0.0).astype(BF)
    partial = jnp.dot(high, fold, preferred_element_type=F32) + jnp.dot(
        low, fold, preferred_element_type=F32
    )
    partial_ref[...] = partial
    sent_ref[...] = partial.astype(BF)


def choose_kernel(subset_ref, _, projector_ref, chosen_ref, sems):
    copies = []
    for part in range(8):
        rows = pl.ds(part * 1024, 1024)
        source = projector_ref.at[subset_ref[0] % SUBSETS, rows]
        copies.append(pltpu.make_async_copy(source, chosen_ref.at[rows], sems.at[part]))
        copies[-1].start()
    for copy in copies:
        copy.wait()


def back_kernel(
    subset_ref,
    measured_ref,
    sinogram_ref,
    axial_ref,
    chosen_ref,
    corrected_ref,
    residual_ref,
    held_ref,
):
    residual = measured_ref[...] - sinogram_ref[...]
    held_ref[...] = residual
    unfold = jnp.where(iota((128, 1024), 1) // 8 == iota((128, 1024), 0), 1.0, 0.0).astype(BF)
    wide = jnp.dot(residual.astype(BF), unfold, preferred_element_type=F32).astype(BF)
    lane = lax.broadcasted_iota(jnp.int32, (16, 1024), 1) % 8
    zero = jnp.zeros((), BF)
    total = jnp.zeros((128, 256), F32)
    for part in range(8):
        rays = wide[part * 16 : (part + 1) * 16]
        spread = jnp.concatenate([jnp.where(lane == y, rays, zero) for y in range(8)], axis=0)
        total = total + jnp.dot(
            spread, chosen_ref[part * 1024 : (part + 1) * 1024, :], preferred_element_type=F32
        )
    corrected_ref[...] = axial_ref[...] + (relaxation(subset_ref) * total).reshape(8, 16, 256)
    index = lax.axis_index("gy")
    block = held_ref[pl.ds(pl.multiple_of((index // 2) * 16, 16), 16), :]
    residual_ref[...] = jnp.where(index % 2 == 1, block[0:12, 64:128], block[0:12, 0:64])


def inner_kernel(
    timestep_ref, corrected_ref, one_ref, middle_ref, bias_ref, last_ref, inner_ref, *scratch
):
    taps, hidden = scratch[0:CORONAL_PLANES], scratch[CORONAL_PLANES:]
    scale_in, _ = noise_scales(timestep_ref)
    absent = jnp.zeros((HALO, 256), F32)

    def planes(step, carry):
        for k in range(CORONAL_PLANES):
            entry = corrected_ref[step * CORONAL_PLANES + k] * scale_in
            layer_one(spread_entry(entry, absent, absent), range(4, 12), one_ref, taps[k])
        for k in range(CORONAL_PLANES):
            layer_two((4, 6, 8), middle_ref, bias_ref, taps[k], hidden[k], 4)
        for k in range(CORONAL_PLANES):
            inner_ref[step * CORONAL_PLANES + k] = jnp.dot(
                last_ref[:, 256:640], hidden[k][...], preferred_element_type=F32
            )
        return carry

    lax.fori_loop(0, 8 // CORONAL_PLANES, planes, 0)


def coronal_kernel(
    timestep_ref,
    corrected_ref,
    first_ref,
    second_ref,
    inner_ref,
    one_ref,
    middle_ref,
    bias_ref,
    last_ref,
    restored_ref,
    *scratch,
):
    scale_in, scale_out = noise_scales(timestep_ref)
    taps, low, high = scratch[0:CORONAL_PLANES], scratch[CORONAL_PLANES : 2 * CORONAL_PLANES], scratch[2 * CORONAL_PLANES :]
    edges = (*range(0, 6), *range(10, 16))

    def planes(step, carry):
        for k in range(CORONAL_PLANES):
            p = step * CORONAL_PLANES + k
            rows = [ref[p] * scale_in for ref in (corrected_ref, first_ref, second_ref)]
            layer_one(spread_entry(*rows), edges, one_ref, taps[k])
        for k in range(CORONAL_PLANES):
            layer_two((0, 2), middle_ref, bias_ref, taps[k], low[k])
            layer_two((10, 12), middle_ref, bias_ref, taps[k], high[k], 10)
        for k in range(CORONAL_PLANES):
            p = step * CORONAL_PLANES + k
            last = inner_ref[p]
            last = last + jnp.dot(last_ref[:, 0:256], low[k][...], preferred_element_type=F32)
            last = last + jnp.dot(last_ref[:, 640:896], high[k][...], preferred_element_type=F32)
            value = corrected_ref[p] + scale_out * layer_three(16, last)
            for z in range(12):
                restored_ref[z, pl.ds(p, 1), :] = value[z : z + 1, :]
        return carry

    lax.fori_loop(0, 8 // CORONAL_PLANES, planes, 0)


def vmem():
    return pl.BlockSpec(memory_space=pltpu.VMEM)


def hbm():
    return pl.BlockSpec(memory_space=pltpu.HBM)


def smem():
    return pl.BlockSpec(memory_space=pltpu.SMEM)


def params(limit):
    return pltpu.CompilerParams(vmem_limit_bytes=limit << 20)


def inner_pairs(size):
    return [(i, i ^ 1) for i in range(size)]


def outer_pairs(size):
    ups = [(i, i + 1) for i in range(1, size - 1, 2)]
    return ups + [(j, i) for i, j in ups]


def exchange(leading, trailing, axis, ordered):
    size = lax.axis_size(axis)
    odd = lax.axis_index(axis) % 2 == 1
    inner = jnp.where(odd, leading, trailing)
    outer = jnp.where(odd, trailing, leading)
    first = lax.ppermute(inner, axis, inner_pairs(size))
    if ordered:
        first, outer = lax.optimization_barrier((first, outer))
    second = lax.ppermute(outer, axis, outer_pairs(size))
    return first, second


def sum_over_gy(partial, sent, later):
    def partner(value, bits):
        return lax.ppermute(value, "gy", [(i, i ^ bits) for i in range(16)]).astype(F32)

    total = partial + partner(sent, 1)
    sent = total.astype(BF)
    total = total + partner(sent, 2) + partner(sent, 4) + partner(sent, 6)
    sent, later = lax.optimization_barrier((total.astype(BF), later))
    return total + partner(sent, 8), later, sent


def per_device(
    volume,
    projector,
    measured,
    subset,
    timestep,
    axial_in,
    axial_bias_in,
    axial_mid,
    axial_bias_mid,
    axial_out,
    coronal_in,
    coronal_bias_in,
    coronal_mid,
    coronal_bias_mid,
    coronal_out,
):
    first, second = exchange(volume[:, :HALO], volume[:, -HALO:], "gy", False)
    prepared = pl.pallas_call(
        prepare_kernel,
        name="prepare",
        out_shape=tuple(jax.ShapeDtypeStruct(*shape) for shape in weight_shapes(12))
        + (jax.ShapeDtypeStruct((128, 128), F32),),
        in_specs=[vmem()] * 6,
        out_specs=(vmem(),) * 5,
        compiler_params=params(40),
        cost_estimate=pl.CostEstimate(flops=1000000, bytes_accessed=3000000, transcendentals=0),
    )(
        coronal_in[:, :, 0],
        coronal_bias_in[None],
        coronal_bias_mid[None],
        coronal_out[:, 0, :],
        coronal_mid,
        measured.T,
    )
    coronal_weights, turned = prepared[0:4], prepared[4]
    flat_projector = projector.reshape(4, 8192, 256)
    axial, partial, sent = pl.pallas_call(
        axial_kernel,
        name="axial",
        out_shape=(
            jax.ShapeDtypeStruct((8, 16, 256), F32),
            jax.ShapeDtypeStruct((128, 128), F32),
            jax.ShapeDtypeStruct((128, 128), BF),
        ),
        in_specs=[smem()] * 2 + [vmem()] * 8 + [hbm()],
        out_specs=(vmem(),) * 3,
        scratch_shapes=[
            pltpu.VMEM((8192, 256), BF),
            pltpu.VMEM((128, 1024), F32),
            pltpu.SemaphoreType.DMA,
        ]
        + [pltpu.VMEM(*shape) for shape in weight_shapes(8)]
        + network_scratch(8),
        compiler_params=params(60),
    )(
        subset,
        timestep,
        volume,
        first,
        second,
        axial_in[:, :, 0],
        axial_bias_in[None],
        axial_bias_mid[None],
        axial_out[:, 0, :],
        axial_mid,
        flat_projector,
    )
    zero = timestep[0].astype(F32) * 0.0
    partial = lax.optimization_barrier(partial + zero)
    sinogram, axial, sent = sum_over_gy(partial, sent, axial)
    chosen = pl.pallas_call(
        choose_kernel,
        name="choose",
        out_shape=jax.ShapeDtypeStruct((8192, 256), BF),
        in_specs=[smem(), vmem(), hbm()],
        out_specs=vmem(),
        scratch_shapes=[pltpu.SemaphoreType.DMA((8,))],
        compiler_params=params(46),
        cost_estimate=pl.CostEstimate(flops=0, bytes_accessed=8 << 20, transcendentals=0),
    )(subset, sent, flat_projector)
    axial = lax.optimization_barrier(axial + zero)
    corrected, residual = pl.pallas_call(
        back_kernel,
        name="back",
        out_shape=(
            jax.ShapeDtypeStruct((8, 16, 256), F32),
            jax.ShapeDtypeStruct((12, 64), F32),
        ),
        in_specs=[smem()] + [vmem()] * 4,
        out_specs=(vmem(), vmem()),
        scratch_shapes=[pltpu.VMEM((128, 128), F32)],
        compiler_params=params(40),
    )(subset, turned, sinogram, axial, chosen)
    first, second = exchange(corrected[:, :HALO], corrected[:, 12 - HALO : 12], "gz", False)
    taps_scratch = [pltpu.VMEM((16 * 192, 256), BF)] * CORONAL_PLANES
    inner = pl.pallas_call(
        inner_kernel,
        name="inner",
        out_shape=jax.ShapeDtypeStruct((8, 48, 256), F32),
        in_specs=[smem()] + [vmem()] * 5,
        out_specs=vmem(),
        scratch_shapes=taps_scratch + [pltpu.VMEM((6 * 64, 256), BF)] * CORONAL_PLANES,
        compiler_params=params(40),
        cost_estimate=pl.CostEstimate(flops=2000000000, bytes_accessed=2 << 20, transcendentals=0),
    )(timestep, corrected, *coronal_weights)
    restored = pl.pallas_call(
        coronal_kernel,
        name="coronal",
        out_shape=jax.ShapeDtypeStruct((12, 8, 256), F32),
        in_specs=[smem()] + [vmem()] * 8,
        out_specs=vmem(),
        scratch_shapes=taps_scratch + [pltpu.VMEM((256, 256), BF)] * (2 * CORONAL_PLANES),
        compiler_params=params(40),
    )(timestep, corrected, first, second, inner, *coronal_weights)
    return (restored, residual.T)


def solution(mesh):
    in_specs = (
        P("gz", "gy", None),
        P(None, None, "gy", None),
        P(None, "gz"),
    ) + (P(),) * 12
    out_specs = (P("gz", "gy", None), P("gy", "gz"))
    return jax.shard_map(
        per_device, mesh=mesh, in_specs=in_specs, out_specs=out_specs, check_vma=False
    )
```
